128 devices in a mesh: req: 8 (over y, core), exp: 16 (over x, z).
Axes of the slice: x: 4, y: 4, z: 4, core: 2. Of those that a mesh axis runs over, the one named last changes fastest.
Arguments:
- hidden_in: bfloat16 [16384, 2048], P(('req', 'exp')), may hold values from -6 to 6
- qkv: bfloat16 [16384, 6144], P(('req', 'exp'))
- q_gain: float32 [128], replicated, as said below
- k_gain: float32 [128], replicated, as said below
- query_pages: bfloat16 [8, 8, 128, 4096], P('req', None, None, 'exp'), may hold values from -6 to 6
- page_table: int32 [8, 8], P('req'), may hold values from 0 to 7, each once within a row
- doc_lengths: int32 [8, 32], P('req'), may hold values from 1 to 128, 2048 in all within a row
- doc_query: int32 [8, 32], P('req'), may hold values from 0 to 7
- out_weight: bfloat16 [2048, 2048], replicated, may hold values from -0.125 to 0.125
- moe_gain: float32 [2048], replicated, may hold values from 0.5 to 1.5
- routes: int32 [16384, 8], P(('req', 'exp')), may hold values from 0 to 63, all different within a row; in each aligned block of 128 rows (0 to 127, 128 to 255, ...) at most 24 rows name the same one
- route_weight: float32 [16384, 8], P(('req', 'exp')), may hold values from 0.02 to 0.25
- gate_weight: bfloat16 [128, 2048, 512], P(('req', 'exp')), may hold values from -0.125 to 0.125
- up_weight: bfloat16 [128, 2048, 512], P(('req', 'exp')), may hold values from -0.125 to 0.125
- down_weight: bfloat16 [128, 512, 2048], P(('req', 'exp')), may hold values from -0.1875 to 0.1875
- score_weight: float32 [2048], replicated, may hold values from -0.125 to 0.125
Outputs:
- layer_out: bfloat16 [16384, 2048], P(('req', 'exp'))
- doc_scores: float32 [8, 32], P('req')
The draws below stay inside these ranges and needn't reach their ends.
Inputs may be any that keep to these rules, and one draw needn't show every extreme that they name: Among the routes of the rows of one device no expert is named more than 24 times; in every draw some device's rows name some expert exactly 24 times. `doc_lengths`: each group's 32 lengths sum to 2048; the longest of each group is exactly 128. `page_table`: each row is a permutation of the pages. `q_gain`: Positive. `k_gain`: Positive.
All inputs are finite; a program needn't handle non-finite values.
Results may differ from the reference program's by a relative error of at most 0.012.
Values may be sent and summed in bfloat16 or wider, within the bound.
A program may use at most 128 MiB of HBM per device.

```python
import math
import jax
import jax.numpy as jnp
import numpy as np
from jax import lax

D = 2048
HEADS = 16
HD = 128
FF = 1024
TOP = 8
TOK_DEV = 128
DOCS = 32
NQ = 8
PAGE = 128
HALF = 512
EXPERTS = 64
GROUP = 2048
TOKENS = 16384
CAP = 24
N_REQ = 8
N_EXP = 16


def draw_qkv(key, part):
    values = jax.random.normal(key, (TOKENS, 3 * D), jnp.float32)
    return values.astype(jnp.bfloat16)


def draw_q_gain(key, part):
    return jax.random.uniform(jax.random.fold_in(key, 11), (HD,), jnp.float32, 0.6, 1.6)


def draw_k_gain(key, part):
    return jax.random.uniform(jax.random.fold_in(key, 23), (HD,), jnp.float32, 0.6, 1.6)


def touch_ends(array, stream_key, low, largest):
    spot = [jax.random.randint(jax.random.fold_in(stream_key, axis), (), 0, length) for axis, length in enumerate(array.shape)]
    widest = array.shape.index(max(array.shape))
    next_to = spot[:widest] + [(spot[widest] + 1) % array.shape[widest]] + spot[widest + 1:]
    return array.at[tuple(spot)].set(low).at[tuple(next_to)].set(largest)


def block_scale(own_key, dims, split, smallest, top_value):
    def one(position, blocks):
        steps = jax.random.uniform(jax.random.fold_in(jax.random.fold_in(own_key, 6), position), (blocks,), jnp.float32, smallest / len(split), top_value / len(split))
        return jnp.repeat(jnp.exp(steps), dims[position] // blocks).reshape((-1,) + (1,) * (len(dims) - position - 1))

    gain = one(*split[0])
    for cut in split[1:]:
        gain = gain * one(*cut)
    return gain


def profile(count, total, most, lean):
    loads = [(1 << 20) // math.isqrt(rank ** lean) + 1 for rank in range(2, count + 1)]
    spare, counts = total - most - (count - 1), [1] * (count - 1)
    while spare > 0:
        free = [i for i in range(count - 1) if counts[i] < most]
        mass, remaining = sum([loads[i] for i in free]), spare
        for i in free:
            extra = min(most - counts[i], max(1, remaining * loads[i] // mass), spare)
            counts[i] = counts[i] + extra
            spare = spare - extra
    return np.array([most] + counts)


def uneven(rng, amount, total, most, skew):
    if amount == 2:
        one = jax.random.randint(rng, (), max(1, total - most), min(most, total - 1) + 1)
        return jnp.stack([one, total - one])
    sizes = jnp.asarray(profile(amount, total, most, skew), jnp.int32)
    pairs = (amount - 1) // 2
    donor, receiver = sizes[1:1 + 2 * pairs:2], sizes[2:2 + 2 * pairs:2]
    slack = jnp.minimum(donor - 1, most - receiver)
    shifted = jax.random.randint(jax.random.fold_in(rng, 1), (pairs,), 0, 1 << 20) % (slack + 1)
    sizes = sizes.at[1:1 + 2 * pairs:2].set(donor - shifted).at[2:2 + 2 * pairs:2].set(receiver + shifted)
    return sizes[jax.random.permutation(jax.random.fold_in(rng, 2), amount)]


def shared_out(key, own, number, rows, amount, top, reach, lean):
    order = jax.random.permutation(key, amount)
    crowded, ordinary = shares(amount, rows * top, reach, lean, True), shares(amount, rows * top, reach, lean, False)
    places = jnp.arange(amount)

    def named(lengths, turn):
        used = int((lengths > 0).sum())
        fixed = max(1, used // 4)
        passed = fixed + (places - fixed + turn * (used - fixed)) % max(1, amount - fixed)
        return jnp.zeros((amount,), jnp.int32).at[order[jnp.where(places < fixed, places, passed)]].set(jnp.asarray(lengths, jnp.int32))

    lengths = jnp.where(number % 4 == 0, named(crowded, number // 4), named(ordinary, number - number // 4 - 1))
    mixed = jax.random.permutation(jax.random.fold_in(own, 3), amount)
    source_of, sink = mixed[0:amount // 2 * 2:2], mixed[1:amount // 2 * 2:2]
    margin = jnp.minimum(lengths[source_of] - 1, reach - lengths[sink]) // 2
    margin = jnp.where((source_of == order[0]) | (sink == order[0]) | (lengths[sink] == 0), 0, jnp.maximum(margin, 0))
    passed = jax.random.randint(jax.random.fold_in(own, 4), (amount // 2,), 0, 1 << 20) % (margin + 1)
    lengths = lengths.at[source_of].add(-passed).at[sink].add(passed)
    items = jnp.searchsorted(jnp.cumsum(lengths), jnp.arange(rows * top), side="right").astype(jnp.int32)
    table = items.reshape(top, rows).T
    table = table[jax.random.permutation(jax.random.fold_in(own, 1), rows)]
    turn = jax.random.randint(jax.random.fold_in(own, 2), (rows, 1), 0, top)
    return jnp.take_along_axis(table, (jnp.arange(top)[None, :] + turn) % top, axis=1)


def shares(number_of, total, reach, skew, full):
    weights = [(1 << 20) // math.isqrt(standing ** skew) + 1 for standing in range(1, number_of + 1)]
    largest = reach if full else min(reach, max(-(-total // number_of), total * weights[0] // sum(weights)))
    least = 1 if total - largest >= number_of - 1 else 0
    counts, surplus = [largest] + [least] * (number_of - 1), total - largest - least * (number_of - 1)
    while surplus > 0:
        movable = [i for i in range(1, number_of) if counts[i] < largest] or [i for i in range(1, number_of) if counts[i] < reach]
        whole, remaining = sum([weights[i] for i in movable]), surplus
        for i in movable:
            more = min(reach - counts[i], max(1, remaining * weights[i] // whole), surplus)
            counts[i] = counts[i] + more
            surplus = surplus - more
    return np.array(counts)


def bell_draw(key, dims, deviation, most, cuts=(), kind=jnp.bfloat16):
    factor_of = block_scale(key, dims, cuts, -0.22, 0.18) if cuts else 1.0
    values = jax.random.normal(key, dims, jnp.float32) * deviation * factor_of
    return jnp.minimum(jnp.maximum(values, -most), most).astype(kind)


def setup_inputs(seed: int = 0) -> dict:
    key_list = jax.random.split(jax.random.key(seed), 17)
    hidden_in = bell_draw(key_list[0], (TOKENS, D), 1.0, 6.0, ((0, 128),))
    qkv = draw_qkv(jax.random.fold_in(key_list[16], 71), 0)
    q_gain = draw_q_gain(jax.random.fold_in(key_list[16], 71), 0)
    k_gain = draw_k_gain(jax.random.fold_in(key_list[16], 71), 0)
    query_pages = bell_draw(key_list[4], (N_REQ, NQ, PAGE, 2 * D), 1.0, 6.0, ((0, 8), (3, 16)))
    page_table = jax.vmap(lambda own: jax.random.permutation(own, NQ))(jax.random.split(key_list[5], N_REQ)).reshape((N_REQ, NQ)).astype(jnp.int32)
    doc_lengths = jax.vmap(lambda own: uneven(own, DOCS, GROUP, TOK_DEV, 2))(jax.random.split(key_list[6], N_REQ)).reshape((N_REQ, DOCS)).astype(jnp.int32)
    doc_query = touch_ends(jax.random.randint(key_list[7], (N_REQ, DOCS), 0, NQ), jax.random.fold_in(key_list[7], 1), 0, NQ - 1).astype(jnp.int32)
    out_weight = bell_draw(key_list[8], (D, D), D ** -0.5, 0.125)
    moe_gain = jnp.clip(1.0 + 0.1 * jax.random.normal(key_list[9], (D,), jnp.float32), 0.5, 1.5)
    routes_keys = jax.random.split(jax.random.fold_in(key_list[10], 1), TOKENS // TOK_DEV)
    routes_turns = jax.random.permutation(jax.random.fold_in(key_list[10], 3), TOKENS // TOK_DEV)
    routes = jax.vmap(lambda own, number: shared_out(jax.random.fold_in(key_list[10], 2), own, number, TOK_DEV, EXPERTS, TOP, CAP, 2))(routes_keys, routes_turns).reshape((TOKENS, TOP))
    route_weight = jnp.clip(0.02 + 0.23 * jax.random.uniform(key_list[11], (TOKENS, TOP), jnp.float32) ** block_scale(key_list[11], (TOKENS, TOP), ((0, 128),), -0.2, 0.2), 0.02, 0.25)
    gate_weight = bell_draw(key_list[12], (2 * EXPERTS, D, HALF), D ** -0.5, 0.125, ((0, 128),))
    up_weight = bell_draw(key_list[13], (2 * EXPERTS, D, HALF), D ** -0.5, 0.125, ((0, 128),))
    down_weight = bell_draw(key_list[14], (2 * EXPERTS, HALF, D), FF ** -0.5, 0.1875, ((0, 128),))
    score_weight = bell_draw(key_list[15], (D,), D ** -0.5, 0.125, (), jnp.float32)
    return {"hidden_in": hidden_in, "qkv": qkv, "q_gain": q_gain, "k_gain": k_gain, "query_pages": query_pages, "page_table": page_table, "doc_lengths": doc_lengths, "doc_query": doc_query, "out_weight": out_weight, "moe_gain": moe_gain, "routes": routes, "route_weight": route_weight, "gate_weight": gate_weight, "up_weight": up_weight, "down_weight": down_weight, "score_weight": score_weight}


eps = 1e-06
rope_base = 50000.0
neg_fill = -1e+30

def rms_scale(values, gain_vec):
    mean_sq = lax.optimization_barrier(jnp.mean(values * values, axis=-1, keepdims=True))
    return values * lax.rsqrt(mean_sq + eps) * gain_vec

def rotate(values, positions):
    half_dim = values.shape[-1] // 2
    frequency = rope_base ** (-(jnp.arange(half_dim, dtype=jnp.float32) * 2.0 / values.shape[-1]))
    angles = positions.astype(jnp.float32)[:, None] * frequency[None, :]
    cosine = jnp.cos(angles)[:, None, :]
    sine_part = jnp.sin(angles)[:, None, :]
    lower_part = values[..., :half_dim]
    upper_part = values[..., half_dim:]
    return jnp.concatenate([lower_part * cosine - upper_part * sine_part, upper_part * cosine + lower_part * sine_part], axis=-1)

def doc_table(doc_len, positions):
    doc_ends = jnp.cumsum(doc_len, dtype=jnp.int32)
    starts = doc_ends - doc_len
    doc_ids = lax.optimization_barrier(jnp.sum((positions[:, None] >= doc_ends[None, :]).astype(jnp.int32), axis=1, dtype=jnp.int32))
    inside = (positions >= 0) & (positions < doc_ends[-1])
    doc_ids = jnp.where(inside, doc_ids, -1)
    member = doc_ids[:, None] == jnp.arange(doc_len.shape[0], dtype=jnp.int32)[None, :]
    doc_start = lax.optimization_barrier(jnp.sum(jnp.where(member, starts[None, :], 0), axis=1, dtype=jnp.int32))
    return (doc_ids, member, doc_start)

def attend(query_rows, key_rows, value_rows, visible):
    score_scale = query_rows.shape[-1] ** (-0.5)
    scores = jnp.einsum('nhd,khd->hnk', query_rows.astype(jnp.float32), key_rows.astype(jnp.float32), precision=lax.Precision.HIGHEST) * score_scale
    scores = jnp.where(visible[None], scores, neg_fill)
    row_max = lax.optimization_barrier(jnp.max(scores, axis=-1))
    probs = jnp.where(visible[None], jnp.exp(scores - row_max[..., None]), 0.0)
    row_total = lax.optimization_barrier(jnp.sum(probs, axis=-1))
    rounded = lax.optimization_barrier(probs.astype(jnp.bfloat16)).astype(jnp.float32)
    weighted = jnp.einsum('hnk,khd->nhd', rounded, value_rows.astype(jnp.float32), precision=lax.Precision.HIGHEST)
    return (weighted, row_max.T, row_total.T)

def slot_numbers(route_flat, bin_count):
    onehot = (route_flat[:, None] == jnp.arange(bin_count, dtype=jnp.int32)[None, :]).astype(jnp.int32)
    prior_count = jnp.cumsum(onehot, axis=0, dtype=jnp.int32) - onehot
    return lax.optimization_barrier(jnp.sum(prior_count * onehot, axis=1, dtype=jnp.int32))

def reference(hidden_in, qkv, q_gain, k_gain, query_pages, page_table, doc_lengths, doc_query, out_weight, moe_gain, routes, route_weight, gate_weight, up_weight, down_weight, score_weight):
    devices = N_REQ * N_EXP
    group_len = TOK_DEV * N_EXP
    positions = jnp.arange(group_len, dtype=jnp.int32)
    doc_ids, member, doc_start = jax.vmap(lambda doc_len: doc_table(doc_len, positions))(doc_lengths)
    rope_pos = (PAGE + positions[None, :] - doc_start).reshape(-1)
    query_rows = rotate(rms_scale(qkv[:, :D].astype(jnp.float32).reshape(TOKENS, HEADS, HD), q_gain), rope_pos).astype(jnp.bfloat16)
    key_rows = rotate(rms_scale(qkv[:, D:2 * D].astype(jnp.float32).reshape(TOKENS, HEADS, HD), k_gain), rope_pos).astype(jnp.bfloat16)
    value_rows = qkv[:, 2 * D:].reshape(TOKENS, HEADS, HD)
    pad_spec = ((0, 0), (TOK_DEV, TOK_DEV), (0, 0), (0, 0))
    key_pad = jnp.pad(key_rows.reshape(N_REQ, group_len, HEADS, HD), pad_spec)
    value_pad = jnp.pad(value_rows.reshape(N_REQ, group_len, HEADS, HD), pad_spec)
    doc_pad = jnp.pad(doc_ids, ((0, 0), (TOK_DEV, TOK_DEV)), constant_values=-1)
    query_ids = jnp.take_along_axis(doc_query, doc_ids, axis=1)
    page_of_tok = jnp.take_along_axis(page_table, query_ids, axis=1)
    pool = query_pages.reshape(N_REQ, NQ * PAGE, HEADS, 2, HD)
    key_page = jnp.arange(NQ * PAGE, dtype=jnp.int32) // PAGE

    def block_attn(block):
        group_id = block // N_EXP
        column_id = block % N_EXP
        own_query = lax.dynamic_slice_in_dim(query_rows, block * TOK_DEV, TOK_DEV, 0)
        own_keys = lax.dynamic_slice_in_dim(lax.dynamic_index_in_dim(key_pad, group_id, 0, False), column_id * TOK_DEV, 3 * TOK_DEV, 0)
        own_values = lax.dynamic_slice_in_dim(lax.dynamic_index_in_dim(value_pad, group_id, 0, False), column_id * TOK_DEV, 3 * TOK_DEV, 0)
        own_doc = lax.dynamic_slice_in_dim(lax.dynamic_index_in_dim(doc_ids, group_id, 0, False), column_id * TOK_DEV, TOK_DEV, 0)
        win_doc = lax.dynamic_slice_in_dim(lax.dynamic_index_in_dim(doc_pad, group_id, 0, False), column_id * TOK_DEV, 3 * TOK_DEV, 0)
        own_page = lax.dynamic_slice_in_dim(lax.dynamic_index_in_dim(page_of_tok, group_id, 0, False), column_id * TOK_DEV, TOK_DEV, 0)
        group_pool = lax.dynamic_index_in_dim(pool, group_id, 0, False)
        all_keys = jnp.concatenate([group_pool[:, :, 0], own_keys], axis=0)
        all_values = jnp.concatenate([group_pool[:, :, 1], own_values], axis=0)
        visible = jnp.concatenate([key_page[None, :] == own_page[:, None], win_doc[None, :] == own_doc[:, None]], axis=1)
        weighted, row_max, row_total = attend(own_query, all_keys, all_values, visible)
        return (weighted / row_total[..., None]).astype(jnp.bfloat16).reshape(TOK_DEV, D)
    attn = lax.map(block_attn, jnp.arange(devices, dtype=jnp.int32)).reshape(TOKENS, D)
    mixed = jnp.dot(attn, out_weight, preferred_element_type=jnp.float32)
    resid = (hidden_in.astype(jnp.float32) + mixed).astype(jnp.bfloat16)
    normed = rms_scale(resid.astype(jnp.float32), moe_gain).astype(jnp.bfloat16)
    route_blocks = routes.reshape(devices, TOK_DEV * TOP)
    weight_blocks = route_weight.reshape(devices, TOK_DEV * TOP)
    slots = jax.vmap(lambda route_flat: slot_numbers(route_flat, EXPERTS))(route_blocks)
    place = route_blocks * CAP + slots
    token_ids = jnp.broadcast_to((jnp.arange(TOK_DEV * TOP, dtype=jnp.int32) // TOP)[None, :], (devices, TOK_DEV * TOP))
    table = jax.vmap(lambda spots, tokens_of: jnp.full((EXPERTS * CAP,), TOK_DEV, jnp.int32).at[spots].set(tokens_of))(place, token_ids)
    weight_table = jax.vmap(lambda spots, route_w: jnp.zeros((EXPERTS * CAP,), jnp.float32).at[spots].set(route_w))(place, weight_blocks)
    normed_blocks = jnp.concatenate([normed.reshape(devices, TOK_DEV, D), jnp.zeros((devices, 1, D), jnp.bfloat16)], axis=1)
    block_rows = jnp.arange(devices, dtype=jnp.int32)[:, None]

    def expert_step(running, expert_id):
        slot_tokens = lax.dynamic_slice_in_dim(table, expert_id * CAP, CAP, 1)
        slot_weights = lax.dynamic_slice_in_dim(weight_table, expert_id * CAP, CAP, 1)
        token_rows = normed_blocks[block_rows, slot_tokens].reshape(devices * CAP, D)
        summed = jnp.zeros((devices * CAP, D), jnp.float32)
        for side_index in range(2):
            piece_id = 2 * expert_id + side_index
            gate_act = jnp.dot(token_rows, lax.dynamic_index_in_dim(gate_weight, piece_id, 0, False), preferred_element_type=jnp.float32)
            up_act = jnp.dot(token_rows, lax.dynamic_index_in_dim(up_weight, piece_id, 0, False), preferred_element_type=jnp.float32)
            hidden_act = (jax.nn.silu(gate_act) * up_act).astype(jnp.bfloat16)
            piece_out = jnp.dot(hidden_act, lax.dynamic_index_in_dim(down_weight, piece_id, 0, False), preferred_element_type=jnp.float32)
            summed = summed + lax.optimization_barrier(piece_out.astype(jnp.bfloat16)).astype(jnp.float32)
        result = lax.optimization_barrier(summed.astype(jnp.bfloat16)).astype(jnp.float32).reshape(devices, CAP, D)
        running = running.at[block_rows, slot_tokens].add(result * slot_weights[..., None])
        return (running, None)
    combined, unused = lax.scan(expert_step, jnp.zeros((devices, TOK_DEV + 1, D), jnp.float32), jnp.arange(EXPERTS, dtype=jnp.int32))
    layer_out = (resid.astype(jnp.float32) + combined[:, :TOK_DEV].reshape(TOKENS, D)).astype(jnp.bfloat16)
    token_score = jnp.dot(layer_out.astype(jnp.float32), score_weight, precision=lax.Precision.HIGHEST).reshape(N_REQ, group_len)
    doc_sums = jnp.einsum('rg,rgd->rd', token_score, member.astype(jnp.float32), precision=lax.Precision.HIGHEST)
    doc_scores = doc_sums / doc_lengths.astype(jnp.float32)
    return (layer_out, doc_scores)
```

```python
import functools

import jax
import jax.numpy as jnp
import numpy as np
from jax import lax
from jax.experimental import pallas as pl
from jax.experimental.pallas import tpu as pltpu
from jax.sharding import PartitionSpec as P

D = 2048
HEADS = 16
HD = 128
FFH = 512
TOK = 128
DOCS = 32
NQ = 8
PAGE = 128
CAP = 24
LINE = 4
ROWS = LINE * CAP
PLANE = 16
NCH = 4
CH = D // NCH
EPS = 1e-06
ROPE_BASE = 50000.0
NEG = -1e30

F32 = jnp.float32
BF16 = jnp.bfloat16
MESH = pl.DeviceIdType.MESH


def iota(shape, dim):
    return lax.broadcasted_iota(jnp.int32, shape, dim)


def iota_f(shape, dim):
    return iota(shape, dim).astype(F32)


def kernel(
    hidden, qkv, q_gain, k_gain, pages, page_table, doc_len, doc_query, w_out, moe_gain, meta,
    gate_w, up_w, down_w, score_w, freq,
    lay, doc_out,
    head_stage, head_all, attn, attn_stage, wo_buf, gate_b, up_b, down_b, meta_all, tri, rank,
    wrow, sel, wsel, resid, tok, stage, arrive, act, ret, part, part_stage, part_in, dsum,
    head_s, head_r, attn_s, attn_r, wo_sem, meta_s, meta_r, loc_sem, wa_s, wa_r, wb_s, wb_r,
    tok_s, tok_r, disp_s, disp_r, ret_s, ret_r, part_s, part_r, dsum_s, dsum_r,
):
    req = lax.axis_index("req")
    me = lax.axis_index("exp")
    y, core = req // 2, req % 2
    x, z = me // 4, me % 4
    kappa = core == z % 2

    def peer(px, py, pz, pc):
        return (2 * py + pc, 4 * px + pz)

    sibling = (2 * y + (1 - core), me)
    partner = (req, 4 * x + (z + 1 - 2 * (z % 2)))

    barrier = pltpu.get_barrier_semaphore()

    @pl.loop(1, 16)
    def _(i):
        pl.semaphore_signal(barrier, 1, device_id=(req, (me + i) % 16), device_id_type=MESH)

    @pl.loop(1, 4)
    def _(dy):
        @pl.loop(0, 4)
        def _(dx):
            pl.semaphore_signal(
                barrier, 1, device_id=peer((x + dx) % 4, (y + dy) % 4, z, core), device_id_type=MESH
            )

    pl.semaphore_signal(barrier, 1, device_id=sibling, device_id_type=MESH)
    pl.semaphore_wait(barrier, 28)

    def remote(src, dst, send, recv, device):
        return pltpu.make_async_remote_copy(
            src_ref=src, dst_ref=dst, send_sem=send, recv_sem=recv, device_id=device, device_id_type=MESH
        )

    def meta_copy(dz):
        return remote(
            meta_all.at[z], meta_all.at[z], meta_s.at[dz - 1], meta_r.at[dz - 1],
            peer(x, y, (z + dz) % 4, core),
        )

    meta_all[z] = meta[...]
    for dz in range(1, 4):
        meta_copy(dz).start()

    def wo_copy(n):
        return pltpu.make_async_copy(
            w_out.at[:, pl.ds(n * CH, CH)], wo_buf.at[n % 2], wo_sem.at[n % 2]
        )

    wo_copy(0).start()
    wo_copy(1).start()

    len_row = doc_len[...].astype(F32)
    eye = iota((DOCS, DOCS), 0) == iota((DOCS, DOCS), 1)
    len_col = jnp.sum(jnp.where(eye, len_row, 0.0), axis=1, keepdims=True)
    upto = iota((DOCS, DOCS), 0) <= iota((DOCS, DOCS), 1)
    ends = jnp.sum(jnp.where(upto, len_col, 0.0), axis=0, keepdims=True)
    starts = ends - len_row
    eye_q = iota((NQ, NQ), 0) == iota((NQ, NQ), 1)
    page_col = jnp.sum(
        jnp.where(eye_q, page_table[...].astype(F32), 0.0), axis=1, keepdims=True
    )
    page_row = jnp.sum(
        jnp.where(doc_query[...] == iota((NQ, DOCS), 0), page_col, 0.0), axis=0, keepdims=True
    )

    def positions(block):
        return (block * TOK).astype(F32) + iota_f((TOK, 1), 0)

    own_pos = positions(me)
    own_start = jnp.max(jnp.where(starts <= own_pos, starts, 0.0), axis=1, keepdims=True)
    angles = (PAGE + own_pos - own_start) * freq[...]
    cosine = jnp.cos(angles)
    sine = jnp.sin(angles)
    sine = jnp.where(iota((TOK, HD), 1) < HD // 2, -sine, sine)

    def norm_rope(values, gain):
        values = values.astype(F32)
        mean_sq = jnp.mean(values * values, axis=-1, keepdims=True)
        values = values * lax.rsqrt(mean_sq + EPS) * gain[...]
        return (values * cosine + pltpu.roll(values, HD // 2, 1) * sine).astype(BF16)

    def head_copy(head):
        return remote(
            head_stage.at[head], head_all.at[me], head_s.at[head], head_r.at[me], (req, head)
        )

    @pl.loop(1, 17)
    def _(i):
        head = (me + i) % 16
        col = pl.multiple_of(head * HD, HD)
        head_stage[head, :, 0:HD] = norm_rope(qkv[:, pl.ds(col, HD)], q_gain)
        head_stage[head, :, HD : 2 * HD] = norm_rope(qkv[:, pl.ds(D + col, HD)], k_gain)
        head_stage[head, :, 2 * HD : 3 * HD] = qkv[:, pl.ds(2 * D + col, HD)]

        @pl.when(i < 16)
        def _():
            head_copy(head).start()

    head_all[me] = head_stage[me]

    weights = ((gate_w, gate_b), (up_w, up_b), (down_w, down_b))

    def local_weight(n):
        return pltpu.make_async_copy(weights[n][0].at[0], weights[n][1].at[0], loc_sem.at[n])

    def first_weight(n):
        return remote(
            weights[n][0].at[0], weights[n][1].at[0], wa_s.at[n], wa_r.at[n], sibling
        )

    def cross_weight(n):
        return remote(
            weights[n][0].at[0], weights[n][1].at[1], wa_s.at[n], wb_r.at[n], partner
        )

    def second_weight(n):
        return remote(
            weights[n][1].at[1], weights[n][1].at[1], wb_s.at[n], wb_r.at[n], sibling
        )

    @pl.when(kappa)
    def _():
        for n in range(3):
            local_weight(n).start()
            first_weight(n).start()

    @pl.when(jnp.logical_not(kappa))
    def _():
        for n in range(3):
            cross_weight(n).start()

    for dz in range(1, 4):
        src = (z - dz + 4) % 4
        remote(
            meta_all.at[src], meta_all.at[src], meta_s.at[dz - 1], meta_r.at[dz - 1], sibling
        ).wait_recv()
    slot = iota((PLANE, 1), 0)
    to_x = (slot % 4 + x) % 4
    to_y = (slot % 4 + slot // 4 + y) % 4
    expert = ((2 * to_y + z % 2) * 8 + 2 * to_x + z // 2).astype(F32)
    for j in range(LINE):
        mask = jnp.zeros((PLANE, TOK), F32)
        weight = jnp.zeros((PLANE, TOK), F32)
        for n in range(8):
            hit = meta_all[j, n : n + 1, :] == expert
            mask = jnp.where(hit, 1.0, mask)
            weight = jnp.where(hit, meta_all[j, 8 + n : 9 + n, :], weight)
        rank[:, j * TOK : (j + 1) * TOK] = mask
        wrow[:, j * TOK : (j + 1) * TOK] = weight
    tri[...] = jnp.where(
        iota((LINE * TOK, LINE * TOK), 0) < iota((LINE * TOK, LINE * TOK), 1), 1.0, 0.0
    ).astype(BF16)
    mask = rank[...]
    prior = jnp.dot(mask.astype(BF16), tri[...], preferred_element_type=F32)
    rank[...] = jnp.where(mask > 0.0, prior, -1.0)

    @pl.loop(0, PLANE)
    def _(r):
        hit = rank[pl.ds(r, 1), :] == iota_f((ROWS, LINE * TOK), 0)
        rows = pl.ds(pl.multiple_of(r * ROWS, ROWS), ROWS)
        sel[rows, :] = jnp.where(hit, 1.0, 0.0).astype(BF16)
        wsel[rows, :] = jnp.where(hit, wrow[pl.ds(r, 1), :], 0.0).astype(BF16)

    @pl.loop(1, 16)
    def _(i):
        src = (me - i + 16) % 16
        remote(
            head_stage.at[src], head_all.at[src], head_s.at[src], head_r.at[src], sibling
        ).wait_recv()

    page_keys = pages[:, :, 0:HD].reshape(NQ * PAGE, HD)
    page_values = pages[:, :, HD : 2 * HD].reshape(NQ * PAGE, HD)
    my_col = pl.ds(pl.multiple_of(me * HD, HD), HD)

    def attn_copy(block):
        return remote(
            attn_stage.at[block], attn.at[:, my_col], attn_s.at[block], attn_r.at[me], (req, block)
        )

    contract_last = (((1,), (1,)), ((), ()))

    @pl.loop(1, 17)
    def _(i):
        block = (me + i) % 16
        first = jnp.clip(block - 1, 0, 13)
        query = head_all[block, :, 0:HD]
        keys = head_all[pl.ds(first, 3), :, HD : 2 * HD].reshape(3 * TOK, HD)
        values = head_all[pl.ds(first, 3), :, 2 * HD : 3 * HD].reshape(3 * TOK, HD)
        pos = positions(block)
        began = starts <= pos
        left = ends > pos
        start = jnp.max(jnp.where(began, starts, 0.0), axis=1, keepdims=True)
        end = jnp.min(jnp.where(left, ends, 4096.0), axis=1, keepdims=True)
        page = jnp.sum(jnp.where(began & left, page_row, 0.0), axis=1, keepdims=True)
        scale = HD**-0.5
        near = lax.dot_general(query, keys, contract_last, preferred_element_type=F32) * scale
        paged = lax.dot_general(query, page_keys, contract_last, preferred_element_type=F32)
        own = paged[:, 0:PAGE]
        for n in range(1, NQ):
            own = jnp.where(page == float(n), paged[:, n * PAGE : (n + 1) * PAGE], own)
        own = own * scale
        key_pos = (first * TOK).astype(F32) + iota_f((TOK, 3 * TOK), 1)
        visible = (key_pos >= start) & (key_pos < end)
        near = jnp.where(visible, near, NEG)
        top = jnp.maximum(
            jnp.max(near, axis=1, keepdims=True), jnp.max(own, axis=1, keepdims=True)
        )
        near = jnp.where(visible, jnp.exp(near - top), 0.0)
        own = jnp.exp(own - top)
        total = jnp.sum(near, axis=1, keepdims=True) + jnp.sum(own, axis=1, keepdims=True)
        spread = jnp.concatenate(
            [jnp.where(page == float(n), own, 0.0).astype(BF16) for n in range(NQ)], axis=1
        )
        weighted = jnp.dot(near.astype(BF16), values, preferred_element_type=F32)
        weighted = weighted + jnp.dot(spread, page_values, preferred_element_type=F32)
        attn_stage[block] = (weighted / total).astype(BF16)

        @pl.when(i < 16)
        def _():
            attn_copy(block).start()

    attn[:, my_col] = attn_stage[me]

    @pl.loop(1, 16)
    def _(i):
        src = (me - i + 16) % 16
        col = pl.ds(pl.multiple_of(src * HD, HD), HD)
        remote(
            attn_stage.at[src], attn.at[:, col], attn_s.at[src], attn_r.at[src], sibling
        ).wait_recv()

    square = jnp.zeros((TOK, 1), F32)
    for n in range(NCH):
        cols = slice(n * CH, (n + 1) * CH)
        wo_copy(n).wait()
        mixed = jnp.dot(attn[...], wo_buf[n % 2], preferred_element_type=F32)
        summed = (hidden[:, cols].astype(F32) + mixed).astype(BF16)
        resid[:, cols] = summed
        wide = summed.astype(F32)
        square = square + jnp.sum(wide * wide, axis=1, keepdims=True)
        if n + 2 < NCH:
            wo_copy(n + 2).start()
    inverse = lax.rsqrt(square * (1.0 / D) + EPS)
    my_rows = pl.ds(pl.multiple_of(z * TOK, TOK), TOK)

    def tok_copy(c, dz):
        block = tok.at[my_rows, pl.ds(c * CH, CH)]
        return remote(
            block, block, tok_s.at[c, dz - 1], tok_r.at[c, dz - 1], peer(x, y, (z + dz) % 4, core)
        )

    for c in range(NCH):
        cols = slice(c * CH, (c + 1) * CH)
        tok[my_rows, cols] = (resid[:, cols].astype(F32) * inverse * moe_gain[:, cols]).astype(BF16)
        for dz in range(1, 4):
            tok_copy(c, dz).start()

    def row_block(r):
        return pl.ds(pl.multiple_of(r * ROWS, ROWS), ROWS)

    def disp_copy(g, i, c):
        rows = row_block(g * 4 + i)
        cols = pl.ds(c * CH, CH)
        return remote(
            stage.at[rows, cols], arrive.at[rows, cols],
            disp_s.at[g * 4 + i, c], disp_r.at[g * 4 + i, c],
            peer((x + i) % 4, (y + i + g) % 4, z, core),
        )

    def select_rows(g, c):
        rows = pl.ds(pl.multiple_of(g * 4 * ROWS, 4 * ROWS), 4 * ROWS)
        cols = slice(c * CH, (c + 1) * CH)
        picked = jnp.dot(sel[rows, :], tok[:, cols], preferred_element_type=F32)
        stage[rows, cols] = picked.astype(BF16)

    for c in range(NCH):
        cols = slice(c * CH, (c + 1) * CH)
        for dz in range(1, 4):
            rows = pl.ds(pl.multiple_of(((z - dz + 4) % 4) * TOK, TOK), TOK)
            block = tok.at[rows, pl.ds(c * CH, CH)]
            remote(block, block, tok_s.at[c, dz - 1], tok_r.at[c, dz - 1], sibling).wait_recv()
        select_rows(0, c)
        for i in range(1, 4):
            disp_copy(0, i, c).start()
        arrive[0:ROWS, cols] = stage[0:ROWS, cols]

    @pl.loop(1, 4)
    def _(g):
        for c in range(NCH):
            select_rows(g, c)
            for i in range(4):
                disp_copy(g, i, c).start()

    @pl.when(kappa)
    def _():
        for n in range(3):
            cross_weight(n).wait_recv()
            second_weight(n).start()
        for n in range(3):
            local_weight(n).wait()

    @pl.when(jnp.logical_not(kappa))
    def _():
        for n in range(3):
            first_weight(n).wait_recv()
            second_weight(n).wait_recv()

    @pl.loop(0, 4)
    def _(g):
        for i in range(4):
            if i == 0:
                @pl.when(g > 0)
                def _():
                    for c in range(NCH):
                        disp_copy(g, 0, c).wait_recv()
            else:
                for c in range(NCH):
                    disp_copy(g, i, c).wait_recv()
        rows = pl.ds(pl.multiple_of(g * 4 * ROWS, 4 * ROWS), 4 * ROWS)
        for s in range(2):
            gate = jnp.dot(arrive[rows, :], gate_b[s], preferred_element_type=F32)
            up = jnp.dot(arrive[rows, :], up_b[s], preferred_element_type=F32)
            act[rows, s * FFH : (s + 1) * FFH] = (
                gate * (1.0 / (1.0 + jnp.exp(-gate))) * up
            ).astype(BF16)

    def ret_copy(g, i, c):
        rows = row_block(g * 4 + i)
        cols = pl.ds(c * CH, CH)
        return remote(
            arrive.at[rows, cols], ret.at[rows, cols],
            ret_s.at[g * 4 + i, c], ret_r.at[g * 4 + i, c],
            peer((x - i + 4) % 4, (y - i - g + 8) % 4, z, core),
        )

    for c in range(NCH):
        cols = slice(c * CH, (c + 1) * CH)

        @pl.loop(0, 4)
        def _(g):
            rows = pl.ds(pl.multiple_of(g * 4 * ROWS, 4 * ROWS), 4 * ROWS)
            piece = jnp.dot(act[rows, 0:FFH], down_b[0, :, cols], preferred_element_type=F32)
            piece = piece + jnp.dot(
                act[rows, FFH : 2 * FFH], down_b[1, :, cols], preferred_element_type=F32
            )
            arrive[rows, cols] = piece.astype(BF16)
            for i in range(4):
                if i == 0:
                    @pl.when(g > 0)
                    def _():
                        ret_copy(g, 0, c).start()
                else:
                    ret_copy(g, i, c).start()

        ret[0:ROWS, cols] = arrive[0:ROWS, cols]

    def part_copy(c, dz):
        target = (z + dz) % 4
        rows = pl.ds(pl.multiple_of(target * TOK, TOK), TOK)
        return remote(
            part_stage.at[c, rows, :], part_in.at[c, dz - 1],
            part_s.at[c, dz - 1], part_r.at[c, dz - 1], peer(x, y, target, core),
        )

    def combine(c):
        cols = slice(c * CH, (c + 1) * CH)

        @pl.loop(0, 4)
        def _(g):
            for i in range(4):
                if i == 0:
                    @pl.when(g > 0)
                    def _():
                        ret_copy(g, 0, c).wait_recv()
                else:
                    ret_copy(g, i, c).wait_recv()

        sums = lax.dot_general(
            wsel[...], ret[:, cols], (((0,), (0,)), ((), ())), preferred_element_type=F32
        )
        part_stage[c] = sums.astype(BF16)
        for dz in range(1, 4):
            part_copy(c, dz).start()
        part[...] = sums
        return part[my_rows, :]

    def finish(c, own, score):
        cols = slice(c * CH, (c + 1) * CH)
        total = own
        for dz in range(1, 4):
            part_copy(c, dz).wait_recv()
            total = total + part_in[c, dz - 1].astype(F32)
        out = (resid[:, cols].astype(F32) + total).astype(BF16)
        lay[:, cols] = out
        return score + jnp.sum(out.astype(F32) * score_w[:, cols], axis=1, keepdims=True)

    score = jnp.zeros((TOK, 1), F32)
    for c in range(NCH):
        tok_own = combine(c)
        own_sums = tok_own
        if c > 0:
            score = finish(c - 1, previous, score)
        previous = own_sums
    score = finish(NCH - 1, previous, score)

    member = (starts <= own_pos) & (ends > own_pos)
    sums = jnp.sum(jnp.where(member, score, 0.0), axis=0, keepdims=True)
    dsum[me, :, 0:DOCS] = jnp.broadcast_to(sums, (8, DOCS))
    dsum[me, :, DOCS:128] = jnp.zeros((8, 128 - DOCS), F32)

    def dsum_copy(target):
        return remote(dsum.at[me], dsum.at[me], dsum_s.at[target], dsum_r.at[me], (req, target))

    @pl.loop(1, 16)
    def _(i):
        dsum_copy((me + i) % 16).start()

    for dz in range(1, 4):
        meta_copy(dz).wait_send()
    for n in range(3):
        @pl.when(kappa)
        def _():
            first_weight(n).wait_send()
            second_weight(n).wait_send()

        @pl.when(jnp.logical_not(kappa))
        def _():
            cross_weight(n).wait_send()

    @pl.loop(1, 16)
    def _(i):
        head_copy((me + i) % 16).wait_send()
        attn_copy((me + i) % 16).wait_send()

    for c in range(NCH):
        for dz in range(1, 4):
            tok_copy(c, dz).wait_send()
            part_copy(c, dz).wait_send()

        @pl.loop(0, 4)
        def _(g):
            for i in range(4):
                if i == 0:
                    @pl.when(g > 0)
                    def _():
                        disp_copy(g, 0, c).wait_send()
                        ret_copy(g, 0, c).wait_send()
                else:
                    disp_copy(g, i, c).wait_send()
                    ret_copy(g, i, c).wait_send()

    @pl.loop(1, 16)
    def _(i):
        src = (me - i + 16) % 16
        remote(
            dsum.at[src], dsum.at[src], dsum_s.at[src], dsum_r.at[src], sibling
        ).wait_recv()

    whole = dsum[0]
    for n in range(1, 16):
        whole = whole + dsum[n]
    doc_out[...] = whole[0:1, 0:DOCS] / len_row

    @pl.loop(1, 16)
    def _(i):
        dsum_copy((me + i) % 16).wait_send()


def local(
    hidden_in, qkv, q_gain, k_gain, query_pages, page_table, doc_lengths, doc_query, out_weight,
    moe_gain, routes, route_weight, gate_weight, up_weight, down_weight, score_weight,
):
    meta = jnp.concatenate([routes.T.astype(F32), route_weight.T], axis=0)
    half = ROPE_BASE ** (-(np.arange(HD // 2, dtype=np.float32) * 2.0 / HD))
    freq = jnp.asarray(np.concatenate([half, half])[None].astype(np.float32))
    vmem = pl.BlockSpec(memory_space=pltpu.VMEM)
    hbm = pl.BlockSpec(memory_space=pl.ANY)
    dma = pltpu.SemaphoreType.DMA
    call = pl.pallas_call(
        kernel,
        out_shape=(
            jax.ShapeDtypeStruct((TOK, D), BF16),
            jax.ShapeDtypeStruct((1, DOCS), F32),
        ),
        in_specs=[
            vmem, vmem, vmem, vmem, vmem, vmem, vmem, vmem, hbm, vmem, vmem,
            hbm, hbm, hbm, vmem, vmem,
        ],
        out_specs=(vmem, vmem),
        scratch_shapes=[
            pltpu.VMEM((HEADS, TOK, 3 * HD), BF16),
            pltpu.VMEM((HEADS, TOK, 3 * HD), BF16),
            pltpu.VMEM((TOK, D), BF16),
            pltpu.VMEM((HEADS, TOK, HD), BF16),
            pltpu.VMEM((2, D, CH), BF16),
            pltpu.VMEM((2, D, FFH), BF16),
            pltpu.VMEM((2, D, FFH), BF16),
            pltpu.VMEM((2, FFH, D), BF16),
            pltpu.VMEM((LINE, 16, TOK), F32),
            pltpu.VMEM((LINE * TOK, LINE * TOK), BF16),
            pltpu.VMEM((PLANE, LINE * TOK), F32),
            pltpu.VMEM((PLANE, LINE * TOK), F32),
            pltpu.VMEM((PLANE * ROWS, LINE * TOK), BF16),
            pltpu.VMEM((PLANE * ROWS, LINE * TOK), BF16),
            pltpu.VMEM((TOK, D), BF16),
            pltpu.VMEM((LINE * TOK, D), BF16),
            pltpu.VMEM((PLANE * ROWS, D), BF16),
            pltpu.VMEM((PLANE * ROWS, D), BF16),
            pltpu.VMEM((PLANE * ROWS, 2 * FFH), BF16),
            pltpu.VMEM((PLANE * ROWS, D), BF16),
            pltpu.VMEM((LINE * TOK, CH), F32),
            pltpu.VMEM((NCH, LINE * TOK, CH), BF16),
            pltpu.VMEM((NCH, LINE - 1, TOK, CH), BF16),
            pltpu.VMEM((16, 8, 128), F32),
            dma((16,)), dma((16,)), dma((16,)), dma((16,)), dma((2,)),
            dma((3,)), dma((3,)), dma((3,)), dma((3,)), dma((3,)), dma((3,)), dma((3,)),
            dma((NCH, 3)), dma((NCH, 3)),
            dma((PLANE, NCH)), dma((PLANE, NCH)), dma((PLANE, NCH)), dma((PLANE, NCH)),
            dma((NCH, 3)), dma((NCH, 3)), dma((16,)), dma((16,)),
        ],
        compiler_params=pltpu.CompilerParams(
            collective_id=0, has_side_effects=True, vmem_limit_bytes=60 * 1024 * 1024
        ),
        cost_estimate=pl.CostEstimate(
            flops=26_000_000_000, bytes_accessed=20_000_000, transcendentals=3_000_000
        ),
    )
    return call(
        hidden_in, qkv, q_gain[None], k_gain[None], query_pages[0], page_table, doc_lengths,
        doc_query, out_weight, moe_gain[None], meta, gate_weight, up_weight, down_weight,
        score_weight[None], freq,
    )


def solution(mesh):
    rows = P(("req", "exp"), None)
    blocks = P(("req", "exp"), None, None)
    in_specs = (
        rows, rows, P(), P(), P("req", None, None, "exp"), P("req", None), P("req", None),
        P("req", None), P(), P(), rows, rows, blocks, blocks, blocks, P(),
    )
    out_specs = (rows, P("req", None))
    return jax.shard_map(local, mesh=mesh, in_specs=in_specs, out_specs=out_specs, check_vma=False)
```

```python
import functools

import jax
import jax.numpy as jnp
import numpy as np
from jax import lax
from jax.experimental import pallas as pl
from jax.experimental.pallas import tpu as pltpu
from jax.sharding import PartitionSpec as P

D = 2048
HEADS = 16
HD = 128
FFH = 512
TOK = 128
DOCS = 32
NQ = 8
PAGE = 128
CAP = 24
LINE = 4
ROWS = LINE * CAP
PLANE = 16
NCH = 4
CH = D // NCH
EPS = 1e-06
ROPE_BASE = 50000.0
NEG = -1e30

OFFSETS = (
    (1, 2), (3, 2), (2, 1), (2, 3),
    (1, 3), (3, 1), (2, 0), (0, 2),
    (0, 0), (2, 2), (1, 1), (3, 3),
    (1, 0), (3, 0), (0, 1), (0, 3),
)
SELF = OFFSETS.index((0, 0))
OTHERS_THEN_SELF = OFFSETS[:SELF] + OFFSETS[SELF + 1 :] + OFFSETS[SELF : SELF + 1]

F32 = jnp.float32
BF16 = jnp.bfloat16
MESH = pl.DeviceIdType.MESH


def iota(shape, dim):
    return lax.broadcasted_iota(jnp.int32, shape, dim)


def iota_f(shape, dim):
    return iota(shape, dim).astype(F32)


def pick(table, axis, index):
    if isinstance(index, int):
        return table[index][axis]
    value = table[-1][axis]
    for n in range(len(table) - 1):
        value = jnp.where(index == n, table[n][axis], value)
    return value


def kernel(
    hidden, qkv, q_gain, k_gain, pages, page_table, doc_len, doc_query, w_out, moe_gain, routes, route_w,
    gate_w, up_w, down_w, score_w, freq,
    lay, doc_out,
    head_stage, head_all, attn, attn_stage, wo_buf, gate_b, up_b, down_b, meta_all, tri, rank,
    wrow, sel, wsel, resid, tok, stage, arrive, act, ret, part, part_stage, part_in, dsum,
    head_s, head_r, attn_s, attn_r, wo_sem, meta_s, meta_r, loc_sem, wa_s, wa_r, wb_s, wb_r,
    tok_s, tok_r, disp_s, disp_r, ret_s, ret_r, part_s, part_r, dsum_s, dsum_r,
):
    req = lax.axis_index("req")
    me = lax.axis_index("exp")
    y, core = req // 2, req % 2
    x, z = me // 4, me % 4
    kappa = core == z % 2

    def peer(px, py, pz, pc):
        return (2 * py + pc, 4 * px + pz)

    sibling = (2 * y + (1 - core), me)
    partner = (req, 4 * x + (z + 1 - 2 * (z % 2)))

    barrier = pltpu.get_barrier_semaphore()

    @pl.loop(1, 16)
    def _(i):
        pl.semaphore_signal(barrier, 1, device_id=(req, (me + i) % 16), device_id_type=MESH)

    @pl.loop(1, 4)
    def _(dy):
        @pl.loop(0, 4)
        def _(dx):
            pl.semaphore_signal(
                barrier, 1, device_id=peer((x + dx) % 4, (y + dy) % 4, z, core), device_id_type=MESH
            )

    pl.semaphore_signal(barrier, 1, device_id=sibling, device_id_type=MESH)
    pl.semaphore_wait(barrier, 28)

    def remote(src, dst, send, recv, device):
        return pltpu.make_async_remote_copy(
            src_ref=src, dst_ref=dst, send_sem=send, recv_sem=recv, device_id=device, device_id_type=MESH
        )

    weights = ((gate_w, gate_b), (up_w, up_b), (down_w, down_b))

    def local_weight(n):
        return pltpu.make_async_copy(weights[n][0].at[0], weights[n][1].at[0], loc_sem.at[n])

    def first_weight(n):
        return remote(
            weights[n][0].at[0], weights[n][1].at[0], wa_s.at[n], wa_r.at[n], sibling
        )

    def cross_weight(n):
        return remote(
            weights[n][0].at[0], weights[n][1].at[1], wa_s.at[n], wb_r.at[n], partner
        )

    def second_weight(n):
        return remote(
            weights[n][1].at[1], weights[n][1].at[1], wb_s.at[n], wb_r.at[n], sibling
        )

    def meta_copy(dz):
        return remote(
            meta_all.at[z], meta_all.at[z], meta_s.at[dz - 1], meta_r.at[dz - 1],
            peer(x, y, (z + dz) % 4, core),
        )

    identity = jnp.where(iota((TOK, TOK), 0) == iota((TOK, TOK), 1), 1.0, 0.0).astype(BF16)

    def turned(values):
        return lax.dot_general(
            values.astype(BF16), identity, (((0,), (0,)), ((), ())), preferred_element_type=F32
        )

    meta_all[z, 0:8, :] = turned(routes[...].astype(F32))
    meta_all[z, 8:16, :] = turned(route_w[...])
    for dz in range(1, 4):
        meta_copy(dz).start()

    def wo_copy(n):
        return pltpu.make_async_copy(
            w_out.at[:, pl.ds(n * CH, CH)], wo_buf.at[n % 2], wo_sem.at[n % 2]
        )

    wo_copy(0).start()
    wo_copy(1).start()

    len_row = doc_len[...].astype(F32)
    eye = iota((DOCS, DOCS), 0) == iota((DOCS, DOCS), 1)
    len_col = jnp.sum(jnp.where(eye, len_row, 0.0), axis=1, keepdims=True)
    upto = iota((DOCS, DOCS), 0) <= iota((DOCS, DOCS), 1)
    ends = jnp.sum(jnp.where(upto, len_col, 0.0), axis=0, keepdims=True)
    starts = ends - len_row
    eye_q = iota((NQ, NQ), 0) == iota((NQ, NQ), 1)
    page_col = jnp.sum(
        jnp.where(eye_q, page_table[...].astype(F32), 0.0), axis=1, keepdims=True
    )
    page_row = jnp.sum(
        jnp.where(doc_query[...] == iota((NQ, DOCS), 0), page_col, 0.0), axis=0, keepdims=True
    )

    def positions(block):
        return (block * TOK).astype(F32) + iota_f((TOK, 1), 0)

    own_pos = positions(me)
    own_start = jnp.max(jnp.where(starts <= own_pos, starts, 0.0), axis=1, keepdims=True)
    angles = (PAGE + own_pos - own_start) * freq[...]
    cosine = jnp.cos(angles)
    sine = jnp.sin(angles)
    sine = jnp.where(iota((TOK, HD), 1) < HD // 2, -sine, sine)

    def norm_rope(values, gain):
        values = values.astype(F32)
        mean_sq = jnp.mean(values * values, axis=-1, keepdims=True)
        values = values * lax.rsqrt(mean_sq + EPS) * gain[...]
        return (values * cosine + pltpu.roll(values, HD // 2, 1) * sine).astype(BF16)

    def head_copy(head):
        return remote(
            head_stage.at[head], head_all.at[me], head_s.at[head], head_r.at[me], (req, head)
        )

    def plane_member(i):
        return 4 * ((x + pick(OTHERS_THEN_SELF, 0, i)) % 4) + (z + pick(OTHERS_THEN_SELF, 1, i)) % 4

    @pl.loop(0, 16)
    def _(i):
        head = plane_member(i)
        col = pl.multiple_of(head * HD, HD)
        head_stage[head, :, 0:HD] = norm_rope(qkv[:, pl.ds(col, HD)], q_gain)
        head_stage[head, :, HD : 2 * HD] = norm_rope(qkv[:, pl.ds(D + col, HD)], k_gain)
        head_stage[head, :, 2 * HD : 3 * HD] = qkv[:, pl.ds(2 * D + col, HD)]

        @pl.when(i < 15)
        def _():
            head_copy(head).start()

    head_all[me] = head_stage[me]

    @pl.when(kappa)
    def _():
        for n in range(3):
            local_weight(n).start()
            first_weight(n).start()

    for dz in range(1, 4):
        src = (z - dz + 4) % 4
        remote(
            meta_all.at[src], meta_all.at[src], meta_s.at[dz - 1], meta_r.at[dz - 1], sibling
        ).wait_recv()
    slot = iota((PLANE, 1), 0)
    to_x = (pick(OFFSETS, 0, slot) + x) % 4
    to_y = (pick(OFFSETS, 1, slot) + y) % 4
    expert = ((2 * to_y + z % 2) * 8 + 2 * to_x + z // 2).astype(F32)
    for j in range(LINE):
        mask = jnp.zeros((PLANE, TOK), F32)
        weight = jnp.zeros((PLANE, TOK), F32)
        for n in range(8):
            hit = meta_all[j, n : n + 1, :] == expert
            mask = jnp.where(hit, 1.0, mask)
            weight = jnp.where(hit, meta_all[j, 8 + n : 9 + n, :], weight)
        rank[:, j * TOK : (j + 1) * TOK] = mask
        wrow[:, j * TOK : (j + 1) * TOK] = weight
    tri[...] = jnp.where(
        iota((LINE * TOK, LINE * TOK), 0) < iota((LINE * TOK, LINE * TOK), 1), 1.0, 0.0
    ).astype(BF16)
    mask = rank[...]
    prior = jnp.dot(mask.astype(BF16), tri[...], preferred_element_type=F32)
    rank[...] = jnp.where(mask > 0.0, prior, -1.0)

    @pl.loop(0, PLANE)
    def _(r):
        hit = rank[pl.ds(r, 1), :] == iota_f((ROWS, LINE * TOK), 0)
        rows = pl.ds(pl.multiple_of(r * ROWS, ROWS), ROWS)
        sel[rows, :] = jnp.where(hit, 1.0, 0.0).astype(BF16)
        wsel[rows, :] = jnp.where(hit, wrow[pl.ds(r, 1), :], 0.0).astype(BF16)

    @pl.loop(1, 16)
    def _(i):
        src = (me - i + 16) % 16
        remote(
            head_stage.at[src], head_all.at[src], head_s.at[src], head_r.at[src], sibling
        ).wait_recv()

    page_keys = pages[:, :, 0:HD].reshape(NQ * PAGE, HD)
    page_values = pages[:, :, HD : 2 * HD].reshape(NQ * PAGE, HD)
    my_col = pl.ds(pl.multiple_of(me * HD, HD), HD)

    def attn_copy(block):
        return remote(
            attn_stage.at[block], attn.at[:, my_col], attn_s.at[block], attn_r.at[me], (req, block)
        )

    contract_last = (((1,), (1,)), ((), ()))

    @pl.loop(0, 16)
    def _(i):
        block = plane_member(i)
        first = jnp.clip(block - 1, 0, 13)
        query = head_all[block, :, 0:HD]
        keys = head_all[pl.ds(first, 3), :, HD : 2 * HD].reshape(3 * TOK, HD)
        values = head_all[pl.ds(first, 3), :, 2 * HD : 3 * HD].reshape(3 * TOK, HD)
        pos = positions(block)
        began = starts <= pos
        left = ends > pos
        start = jnp.max(jnp.where(began, starts, 0.0), axis=1, keepdims=True)
        end = jnp.min(jnp.where(left, ends, 4096.0), axis=1, keepdims=True)
        page = jnp.sum(jnp.where(began & left, page_row, 0.0), axis=1, keepdims=True)
        scale = HD**-0.5
        near = lax.dot_general(query, keys, contract_last, preferred_element_type=F32) * scale
        paged = lax.dot_general(query, page_keys, contract_last, preferred_element_type=F32)
        own = paged[:, 0:PAGE]
        for n in range(1, NQ):
            own = jnp.where(page == float(n), paged[:, n * PAGE : (n + 1) * PAGE], own)
        own = own * scale
        key_pos = (first * TOK).astype(F32) + iota_f((TOK, 3 * TOK), 1)
        visible = (key_pos >= start) & (key_pos < end)
        near = jnp.where(visible, near, NEG)
        top = jnp.maximum(
            jnp.max(near, axis=1, keepdims=True), jnp.max(own, axis=1, keepdims=True)
        )
        near = jnp.where(visible, jnp.exp(near - top), 0.0)
        own = jnp.exp(own - top)
        total = jnp.sum(near, axis=1, keepdims=True) + jnp.sum(own, axis=1, keepdims=True)
        spread = jnp.concatenate(
            [jnp.where(page == float(n), own, 0.0).astype(BF16) for n in range(NQ)], axis=1
        )
        weighted = jnp.dot(near.astype(BF16), values, preferred_element_type=F32)
        weighted = weighted + jnp.dot(spread, page_values, preferred_element_type=F32)
        attn_stage[block] = (weighted / total).astype(BF16)

        @pl.when(i < 15)
        def _():
            attn_copy(block).start()

    attn[:, my_col] = attn_stage[me]

    @pl.loop(1, 16)
    def _(i):
        src = (me - i + 16) % 16
        col = pl.ds(pl.multiple_of(src * HD, HD), HD)
        remote(
            attn_stage.at[src], attn.at[:, col], attn_s.at[src], attn_r.at[src], sibling
        ).wait_recv()

    square = jnp.zeros((TOK, 1), F32)
    for n in range(NCH):
        cols = slice(n * CH, (n + 1) * CH)
        wo_copy(n).wait()
        mixed = jnp.dot(attn[...], wo_buf[n % 2], preferred_element_type=F32)
        summed = (hidden[:, cols].astype(F32) + mixed).astype(BF16)
        resid[:, cols] = summed
        wide = summed.astype(F32)
        square = square + jnp.sum(wide * wide, axis=1, keepdims=True)
        if n + 2 < NCH:
            wo_copy(n + 2).start()
    inverse = lax.rsqrt(square * (1.0 / D) + EPS)
    my_rows = pl.ds(pl.multiple_of(z * TOK, TOK), TOK)

    def tok_copy(c, dz):
        block = tok.at[my_rows, pl.ds(c * CH, CH)]
        return remote(
            block, block, tok_s.at[c, dz - 1], tok_r.at[c, dz - 1], peer(x, y, (z + dz) % 4, core)
        )

    for c in range(NCH):
        cols = slice(c * CH, (c + 1) * CH)
        tok[my_rows, cols] = (resid[:, cols].astype(F32) * inverse * moe_gain[:, cols]).astype(BF16)
        for dz in (1, 3, 2):
            tok_copy(c, dz).start()

    @pl.when(jnp.logical_not(kappa))
    def _():
        for n in range(3):
            cross_weight(n).start()

    def row_block(r):
        return pl.ds(pl.multiple_of(r * ROWS, ROWS), ROWS)

    def disp_copy(r, c):
        rows = row_block(r)
        cols = pl.ds(c * CH, CH)
        return remote(
            stage.at[rows, cols], arrive.at[rows, cols], disp_s.at[r, c], disp_r.at[r, c],
            peer((x + pick(OFFSETS, 0, r)) % 4, (y + pick(OFFSETS, 1, r)) % 4, z, core),
        )

    def select_rows(g, c):
        rows = pl.ds(pl.multiple_of(g * 4 * ROWS, 4 * ROWS), 4 * ROWS)
        cols = slice(c * CH, (c + 1) * CH)
        picked = jnp.dot(sel[rows, :], tok[:, cols], preferred_element_type=F32)
        stage[rows, cols] = picked.astype(BF16)

    def not_self(r, action):
        if isinstance(r, int):
            if r != SELF:
                action()
        else:
            pl.when(r != SELF)(action)

    def disp_group(g, act_on):
        for i in range(4):
            def action(r=g * 4 + i):
                for c in range(NCH):
                    act_on(disp_copy(r, c))

            not_self(g * 4 + i, action)

    for c in range(NCH):
        cols = slice(c * CH, (c + 1) * CH)
        for dz in range(1, 4):
            rows = pl.ds(pl.multiple_of(((z - dz + 4) % 4) * TOK, TOK), TOK)
            block = tok.at[rows, pl.ds(c * CH, CH)]
            remote(block, block, tok_s.at[c, dz - 1], tok_r.at[c, dz - 1], sibling).wait_recv()
        select_rows(0, c)
        for i in range(4):
            disp_copy(i, c).start()

    @pl.loop(1, 4)
    def _(g):
        for c in range(NCH):
            select_rows(g, c)
            for i in range(4):
                not_self(g * 4 + i, lambda r=g * 4 + i: disp_copy(r, c).start())

    self_rows = slice(SELF * ROWS, (SELF + 1) * ROWS)
    arrive[self_rows, :] = stage[self_rows, :]

    def near_weight(n):
        @pl.when(kappa)
        def _():
            local_weight(n).wait()

        @pl.when(jnp.logical_not(kappa))
        def _():
            first_weight(n).wait_recv()

    def far_weight(n):
        @pl.when(kappa)
        def _():
            cross_weight(n).wait_recv()
            second_weight(n).start()

        @pl.when(jnp.logical_not(kappa))
        def _():
            second_weight(n).wait_recv()

    for n in range(2):
        near_weight(n)
        far_weight(n)

    @pl.loop(0, 4)
    def _(g):
        disp_group(g, lambda copy: copy.wait_recv())
        rows = pl.ds(pl.multiple_of(g * 4 * ROWS, 4 * ROWS), 4 * ROWS)
        for s in range(2):
            gate = jnp.dot(arrive[rows, :], gate_b[s], preferred_element_type=F32)
            up = jnp.dot(arrive[rows, :], up_b[s], preferred_element_type=F32)
            act[rows, s * FFH : (s + 1) * FFH] = (
                gate * (1.0 / (1.0 + jnp.exp(-gate))) * up
            ).astype(BF16)

    def ret_copy(r, c):
        rows = row_block(r)
        cols = pl.ds(c * CH, CH)
        return remote(
            arrive.at[rows, cols], ret.at[rows, cols], ret_s.at[r, c], ret_r.at[r, c],
            peer((x - pick(OFFSETS, 0, r) + 4) % 4, (y - pick(OFFSETS, 1, r) + 4) % 4, z, core),
        )

    def ret_chunk(c, act_on):
        @pl.loop(0, PLANE)
        def _(r):
            not_self(r, lambda: act_on(ret_copy(r, c)))

    def down_rows(c):
        cols = slice(c * CH, (c + 1) * CH)

        @pl.loop(0, 4)
        def _(g):
            rows = pl.ds(pl.multiple_of(g * 4 * ROWS, 4 * ROWS), 4 * ROWS)
            piece = jnp.dot(act[rows, 0:FFH], down_b[0, :, cols], preferred_element_type=F32)
            piece = piece + jnp.dot(
                act[rows, FFH : 2 * FFH], down_b[1, :, cols], preferred_element_type=F32
            )
            arrive[rows, cols] = piece.astype(BF16)

        ret[self_rows, cols] = arrive[self_rows, cols]

    def part_copy(c, dz):
        target = (z + dz) % 4
        rows = pl.ds(pl.multiple_of(target * TOK, TOK), TOK)
        return remote(
            part_stage.at[c, rows, :], part_in.at[c, dz - 1],
            part_s.at[c, dz - 1], part_r.at[c, dz - 1], peer(x, y, target, core),
        )

    def combine(c):
        cols = slice(c * CH, (c + 1) * CH)

        ret_chunk(c, lambda copy: copy.wait_recv())
        sums = lax.dot_general(
            wsel[...], ret[:, cols], (((0,), (0,)), ((), ())), preferred_element_type=F32
        )
        part_stage[c] = sums.astype(BF16)
        for dz in (1, 3, 2):
            part_copy(c, dz).start()
        part[...] = sums
        return part[my_rows, :]

    def finish(c, own, score):
        cols = slice(c * CH, (c + 1) * CH)
        total = own
        for dz in range(1, 4):
            part_copy(c, dz).wait_recv()
            total = total + part_in[c, dz - 1].astype(F32)
        out = (resid[:, cols].astype(F32) + total).astype(BF16)
        lay[:, cols] = out
        return score + jnp.sum(out.astype(F32) * score_w[:, cols], axis=1, keepdims=True)

    def send_back(c):
        ret_chunk(c, lambda copy: copy.start())

    def sent_back(c):
        ret_chunk(c, lambda copy: copy.wait_send())

    near_weight(2)
    far_weight(2)
    score = jnp.zeros((TOK, 1), F32)
    down_rows(0)
    send_back(0)
    down_rows(1)
    send_back(1)
    down_rows(2)
    sent_back(0)
    send_back(2)
    own_0 = combine(0)
    down_rows(3)
    sent_back(1)
    send_back(3)
    own_1 = combine(1)
    score = finish(0, own_0, score)
    own_2 = combine(2)
    score = finish(1, own_1, score)
    own_3 = combine(3)
    score = finish(2, own_2, score)
    score = finish(3, own_3, score)

    member = (starts <= own_pos) & (ends > own_pos)
    sums = jnp.sum(jnp.where(member, score, 0.0), axis=0, keepdims=True)
    dsum[me, :, 0:DOCS] = jnp.broadcast_to(sums, (8, DOCS))
    dsum[me, :, DOCS:128] = jnp.zeros((8, 128 - DOCS), F32)

    def dsum_copy(target):
        return remote(dsum.at[me], dsum.at[me], dsum_s.at[target], dsum_r.at[me], (req, target))

    @pl.loop(1, 16)
    def _(i):
        dsum_copy((me + i) % 16).start()

    for dz in range(1, 4):
        meta_copy(dz).wait_send()
    for n in range(3):
        @pl.when(kappa)
        def _():
            first_weight(n).wait_send()
            second_weight(n).wait_send()

        @pl.when(jnp.logical_not(kappa))
        def _():
            cross_weight(n).wait_send()

    @pl.loop(1, 16)
    def _(i):
        head_copy((me + i) % 16).wait_send()
        attn_copy((me + i) % 16).wait_send()

    for c in range(NCH):
        for dz in range(1, 4):
            tok_copy(c, dz).wait_send()
            part_copy(c, dz).wait_send()

    @pl.loop(0, 4)
    def _(g):
        disp_group(g, lambda copy: copy.wait_send())

    sent_back(2)
    sent_back(3)

    @pl.loop(1, 16)
    def _(i):
        src = (me - i + 16) % 16
        remote(
            dsum.at[src], dsum.at[src], dsum_s.at[src], dsum_r.at[src], sibling
        ).wait_recv()

    whole = dsum[0]
    for n in range(1, 16):
        whole = whole + dsum[n]
    doc_out[...] = whole[0:1, 0:DOCS] / len_row

    @pl.loop(1, 16)
    def _(i):
        dsum_copy((me + i) % 16).wait_send()


def local(
    hidden_in, qkv, q_gain, k_gain, query_pages, page_table, doc_lengths, doc_query, out_weight,
    moe_gain, routes, route_weight, gate_weight, up_weight, down_weight, score_weight,
):
    half = ROPE_BASE ** (-(np.arange(HD // 2, dtype=np.float32) * 2.0 / HD))
    freq = jnp.asarray(np.concatenate([half, half])[None].astype(np.float32))
    vmem = pl.BlockSpec(memory_space=pltpu.VMEM)
    hbm = pl.BlockSpec(memory_space=pl.ANY)
    dma = pltpu.SemaphoreType.DMA
    call = pl.pallas_call(
        kernel,
        out_shape=(
            jax.ShapeDtypeStruct((TOK, D), BF16),
            jax.ShapeDtypeStruct((1, DOCS), F32),
        ),
        in_specs=[
            vmem, vmem, vmem, vmem, vmem, vmem, vmem, vmem, hbm, vmem, vmem, vmem,
            hbm, hbm, hbm, vmem, vmem,
        ],
        out_specs=(vmem, vmem),
        scratch_shapes=[
            pltpu.VMEM((HEADS, TOK, 3 * HD), BF16),
            pltpu.VMEM((HEADS, TOK, 3 * HD), BF16),
            pltpu.VMEM((TOK, D), BF16),
            pltpu.VMEM((HEADS, TOK, HD), BF16),
            pltpu.VMEM((2, D, CH), BF16),
            pltpu.VMEM((2, D, FFH), BF16),
            pltpu.VMEM((2, D, FFH), BF16),
            pltpu.VMEM((2, FFH, D), BF16),
            pltpu.VMEM((LINE, 16, TOK), F32),
            pltpu.VMEM((LINE * TOK, LINE * TOK), BF16),
            pltpu.VMEM((PLANE, LINE * TOK), F32),
            pltpu.VMEM((PLANE, LINE * TOK), F32),
            pltpu.VMEM((PLANE * ROWS, LINE * TOK), BF16),
            pltpu.VMEM((PLANE * ROWS, LINE * TOK), BF16),
            pltpu.VMEM((TOK, D), BF16),
            pltpu.VMEM((LINE * TOK, D), BF16),
            pltpu.VMEM((PLANE * ROWS, D), BF16),
            pltpu.VMEM((PLANE * ROWS, D), BF16),
            pltpu.VMEM((PLANE * ROWS, 2 * FFH), BF16),
            pltpu.VMEM((PLANE * ROWS, D), BF16),
            pltpu.VMEM((LINE * TOK, CH), F32),
            pltpu.VMEM((NCH, LINE * TOK, CH), BF16),
            pltpu.VMEM((NCH, LINE - 1, TOK, CH), BF16),
            pltpu.VMEM((16, 8, 128), F32),
            dma((16,)), dma((16,)), dma((16,)), dma((16,)), dma((2,)),
            dma((3,)), dma((3,)), dma((3,)), dma((3,)), dma((3,)), dma((3,)), dma((3,)),
            dma((NCH, 3)), dma((NCH, 3)),
            dma((PLANE, NCH)), dma((PLANE, NCH)), dma((PLANE, NCH)), dma((PLANE, NCH)),
            dma((NCH, 3)), dma((NCH, 3)), dma((16,)), dma((16,)),
        ],
        compiler_params=pltpu.CompilerParams(
            collective_id=0, has_side_effects=True, vmem_limit_bytes=60 * 1024 * 1024
        ),
        cost_estimate=pl.CostEstimate(
            flops=26_000_000_000, bytes_accessed=20_000_000, transcendentals=3_000_000
        ),
    )
    return call(
        hidden_in, qkv, q_gain[None], k_gain[None], query_pages[0], page_table, doc_lengths,
        doc_query, out_weight, moe_gain[None], routes, route_weight, gate_weight, up_weight, down_weight,
        score_weight[None], freq,
    )


def solution(mesh):
    rows = P(("req", "exp"), None)
    blocks = P(("req", "exp"), None, None)
    in_specs = (
        rows, rows, P(), P(), P("req", None, None, "exp"), P("req", None), P("req", None),
        P("req", None), P(), P(), rows, rows, blocks, blocks, blocks, P(),
    )
    out_specs = (rows, P("req", None))
    return jax.shard_map(local, mesh=mesh, in_specs=in_specs, out_specs=out_specs, check_vma=False)
```

```python
import functools

import jax
import jax.numpy as jnp
import numpy as np
from jax import lax
from jax.experimental import pallas as pl
from jax.experimental.pallas import tpu as pltpu
from jax.sharding import PartitionSpec as P

D = 2048
HEADS = 16
HD = 128
FFH = 512
TOK = 128
DOCS = 32
NQ = 8
PAGE = 128
CAP = 24
LINE = 4
ROWS = LINE * CAP
PLANE = 16
NCH = 4
CH = D // NCH
EPS = 1e-06
ROPE_BASE = 50000.0
NEG = -1e30

OFFSETS = (
    (1, 2), (3, 2), (2, 1), (2, 3),
    (1, 3), (3, 1), (2, 0), (0, 2),
    (0, 0), (2, 2), (1, 1), (3, 3),
    (1, 0), (3, 0), (0, 1), (0, 3),
)
SELF = OFFSETS.index((0, 0))
OTHERS_THEN_SELF = OFFSETS[:SELF] + OFFSETS[SELF + 1 :] + OFFSETS[SELF : SELF + 1]

F32 = jnp.float32
BF16 = jnp.bfloat16
MESH = pl.DeviceIdType.MESH


def iota(shape, dim):
    return lax.broadcasted_iota(jnp.int32, shape, dim)


def iota_f(shape, dim):
    return iota(shape, dim).astype(F32)


def pick(table, axis, index):
    if isinstance(index, int):
        return table[index][axis]
    value = table[-1][axis]
    for n in range(len(table) - 1):
        value = jnp.where(index == n, table[n][axis], value)
    return value


def kernel(
    hidden, qkv, q_gain, k_gain, pages, page_table, doc_len, doc_query, w_out, moe_gain, routes, route_w,
    gate_w, up_w, down_w, score_w, freq,
    lay, doc_out,
    head_stage, head_all, attn, attn_stage, wo_buf, gate_b, up_b, down_b, meta_all, tri, rank,
    wrow, sel, wsel, resid, tok, stage, arrive, act, ret, part, part_stage, part_in, dsum,
    head_s, head_r, attn_s, attn_r, wo_sem, meta_s, meta_r, loc_sem, wa_s, wa_r, wb_s, wb_r,
    tok_s, tok_r, disp_s, disp_r, ret_s, ret_r, part_s, part_r, dsum_s, dsum_r,
):
    req = lax.axis_index("req")
    me = lax.axis_index("exp")
    y, core = req // 2, req % 2
    x, z = me // 4, me % 4
    kappa = core == z % 2

    def peer(px, py, pz, pc):
        return (2 * py + pc, 4 * px + pz)

    sibling = (2 * y + (1 - core), me)
    partner = (req, 4 * x + (z + 1 - 2 * (z % 2)))

    barrier = pltpu.get_barrier_semaphore()

    @pl.loop(1, 16)
    def _(i):
        pl.semaphore_signal(barrier, 1, device_id=(req, (me + i) % 16), device_id_type=MESH)

    @pl.loop(1, 4)
    def _(dy):
        @pl.loop(0, 4)
        def _(dx):
            pl.semaphore_signal(
                barrier, 1, device_id=peer((x + dx) % 4, (y + dy) % 4, z, core), device_id_type=MESH
            )

    pl.semaphore_signal(barrier, 1, device_id=sibling, device_id_type=MESH)
    pl.semaphore_wait(barrier, 28)

    def remote(src, dst, send, recv, device):
        return pltpu.make_async_remote_copy(
            src_ref=src, dst_ref=dst, send_sem=send, recv_sem=recv, device_id=device, device_id_type=MESH
        )

    weights = ((gate_w, gate_b), (up_w, up_b), (down_w, down_b))

    def local_weight(n):
        return pltpu.make_async_copy(weights[n][0].at[0], weights[n][1].at[0], loc_sem.at[n])

    def first_weight(n):
        return remote(
            weights[n][0].at[0], weights[n][1].at[0], wa_s.at[n], wa_r.at[n], sibling
        )

    def cross_weight(n):
        return remote(
            weights[n][0].at[0], weights[n][1].at[1], wa_s.at[n], wb_r.at[n], partner
        )

    def second_weight(n):
        return remote(
            weights[n][1].at[1], weights[n][1].at[1], wb_s.at[n], wb_r.at[n], sibling
        )

    def meta_copy(dz):
        return remote(
            meta_all.at[z], meta_all.at[z], meta_s.at[dz - 1], meta_r.at[dz - 1],
            peer(x, y, (z + dz) % 4, core),
        )

    identity = jnp.where(iota((TOK, TOK), 0) == iota((TOK, TOK), 1), 1.0, 0.0).astype(BF16)

    def turned(values):
        return lax.dot_general(
            values.astype(BF16), identity, (((0,), (0,)), ((), ())), preferred_element_type=F32
        )

    meta_all[z, 0:8, :] = turned(routes[...].astype(F32))
    meta_all[z, 8:16, :] = turned(route_w[...])
    for dz in range(1, 4):
        meta_copy(dz).start()

    def wo_copy(n):
        return pltpu.make_async_copy(
            w_out.at[:, pl.ds(n * CH, CH)], wo_buf.at[n % 2], wo_sem.at[n % 2]
        )

    wo_copy(0).start()
    wo_copy(1).start()

    len_row = doc_len[...].astype(F32)
    eye = iota((DOCS, DOCS), 0) == iota((DOCS, DOCS), 1)
    len_col = jnp.sum(jnp.where(eye, len_row, 0.0), axis=1, keepdims=True)
    upto = iota((DOCS, DOCS), 0) <= iota((DOCS, DOCS), 1)
    ends = jnp.sum(jnp.where(upto, len_col, 0.0), axis=0, keepdims=True)
    starts = ends - len_row
    eye_q = iota((NQ, NQ), 0) == iota((NQ, NQ), 1)
    page_col = jnp.sum(
        jnp.where(eye_q, page_table[...].astype(F32), 0.0), axis=1, keepdims=True
    )
    page_row = jnp.sum(
        jnp.where(doc_query[...] == iota((NQ, DOCS), 0), page_col, 0.0), axis=0, keepdims=True
    )

    def positions(block):
        return (block * TOK).astype(F32) + iota_f((TOK, 1), 0)

    own_pos = positions(me)
    own_start = jnp.max(jnp.where(starts <= own_pos, starts, 0.0), axis=1, keepdims=True)
    angles = (PAGE + own_pos - own_start) * freq[...]
    cosine = jnp.cos(angles)
    sine = jnp.sin(angles)
    sine = jnp.where(iota((TOK, HD), 1) < HD // 2, -sine, sine)

    def norm_rope(values, gain):
        values = values.astype(F32)
        mean_sq = jnp.mean(values * values, axis=-1, keepdims=True)
        values = values * lax.rsqrt(mean_sq + EPS) * gain[...]
        return (values * cosine + pltpu.roll(values, HD // 2, 1) * sine).astype(BF16)

    def head_copy(head):
        return remote(
            head_stage.at[head], head_all.at[me], head_s.at[head], head_r.at[me], (req, head)
        )

    def plane_member(i):
        return 4 * ((x + pick(OTHERS_THEN_SELF, 0, i)) % 4) + (z + pick(OTHERS_THEN_SELF, 1, i)) % 4

    @pl.loop(0, 16)
    def _(i):
        head = plane_member(i)
        col = pl.multiple_of(head * HD, HD)
        head_stage[head, :, 0:HD] = norm_rope(qkv[:, pl.ds(col, HD)], q_gain)
        head_stage[head, :, HD : 2 * HD] = norm_rope(qkv[:, pl.ds(D + col, HD)], k_gain)
        head_stage[head, :, 2 * HD : 3 * HD] = qkv[:, pl.ds(2 * D + col, HD)]

        @pl.when(i < 15)
        def _():
            head_copy(head).start()

    head_all[me] = head_stage[me]

    @pl.when(kappa)
    def _():
        for n in range(3):
            local_weight(n).start()
            first_weight(n).start()

    for dz in range(1, 4):
        src = (z - dz + 4) % 4
        remote(
            meta_all.at[src], meta_all.at[src], meta_s.at[dz - 1], meta_r.at[dz - 1], sibling
        ).wait_recv()
    slot = iota((PLANE, 1), 0)
    to_x = (pick(OFFSETS, 0, slot) + x) % 4
    to_y = (pick(OFFSETS, 1, slot) + y) % 4
    expert = ((2 * to_y + z % 2) * 8 + 2 * to_x + z // 2).astype(F32)
    for j in range(LINE):
        mask = jnp.zeros((PLANE, TOK), F32)
        weight = jnp.zeros((PLANE, TOK), F32)
        for n in range(8):
            hit = meta_all[j, n : n + 1, :] == expert
            mask = jnp.where(hit, 1.0, mask)
            weight = jnp.where(hit, meta_all[j, 8 + n : 9 + n, :], weight)
        rank[:, j * TOK : (j + 1) * TOK] = mask
        wrow[:, j * TOK : (j + 1) * TOK] = weight
    tri[...] = jnp.where(
        iota((LINE * TOK, LINE * TOK), 0) < iota((LINE * TOK, LINE * TOK), 1), 1.0, 0.0
    ).astype(BF16)
    mask = rank[...]
    prior = jnp.dot(mask.astype(BF16), tri[...], preferred_element_type=F32)
    rank[...] = jnp.where(mask > 0.0, prior, -1.0)

    @pl.loop(0, PLANE)
    def _(r):
        hit = rank[pl.ds(r, 1), :] == iota_f((ROWS, LINE * TOK), 0)
        rows = pl.ds(pl.multiple_of(r * ROWS, ROWS), ROWS)
        sel[rows, :] = jnp.where(hit, 1.0, 0.0).astype(BF16)
        wsel[rows, :] = jnp.where(hit, wrow[pl.ds(r, 1), :], 0.0).astype(BF16)

    @pl.loop(1, 16)
    def _(i):
        src = (me - i + 16) % 16
        remote(
            head_stage.at[src], head_all.at[src], head_s.at[src], head_r.at[src], sibling
        ).wait_recv()

    page_keys = pages[:, :, 0:HD].reshape(NQ * PAGE, HD)
    page_values = pages[:, :, HD : 2 * HD].reshape(NQ * PAGE, HD)
    my_col = pl.ds(pl.multiple_of(me * HD, HD), HD)

    def attn_copy(block):
        return remote(
            attn_stage.at[block], attn.at[:, my_col], attn_s.at[block], attn_r.at[me], (req, block)
        )

    contract_last = (((1,), (1,)), ((), ()))

    @pl.loop(0, 16)
    def _(i):
        block = plane_member(i)
        first = jnp.clip(block - 1, 0, 13)
        query = head_all[block, :, 0:HD]
        keys = head_all[pl.ds(first, 3), :, HD : 2 * HD].reshape(3 * TOK, HD)
        values = head_all[pl.ds(first, 3), :, 2 * HD : 3 * HD].reshape(3 * TOK, HD)
        pos = positions(block)
        began = starts <= pos
        left = ends > pos
        start = jnp.max(jnp.where(began, starts, 0.0), axis=1, keepdims=True)
        end = jnp.min(jnp.where(left, ends, 4096.0), axis=1, keepdims=True)
        page = jnp.sum(jnp.where(began & left, page_row, 0.0), axis=1, keepdims=True)
        scale = HD**-0.5
        near = lax.dot_general(query, keys, contract_last, preferred_element_type=F32) * scale
        paged = lax.dot_general(query, page_keys, contract_last, preferred_element_type=F32)
        own = paged[:, 0:PAGE]
        for n in range(1, NQ):
            own = jnp.where(page == float(n), paged[:, n * PAGE : (n + 1) * PAGE], own)
        own = own * scale
        key_pos = (first * TOK).astype(F32) + iota_f((TOK, 3 * TOK), 1)
        visible = (key_pos >= start) & (key_pos < end)
        near = jnp.where(visible, near, NEG)
        top = jnp.maximum(
            jnp.max(near, axis=1, keepdims=True), jnp.max(own, axis=1, keepdims=True)
        )
        near = jnp.where(visible, jnp.exp(near - top), 0.0)
        own = jnp.exp(own - top)
        total = jnp.sum(near, axis=1, keepdims=True) + jnp.sum(own, axis=1, keepdims=True)
        spread = jnp.concatenate(
            [jnp.where(page == float(n), own, 0.0).astype(BF16) for n in range(NQ)], axis=1
        )
        weighted = jnp.dot(near.astype(BF16), values, preferred_element_type=F32)
        weighted = weighted + jnp.dot(spread, page_values, preferred_element_type=F32)
        attn_stage[block] = (weighted / total).astype(BF16)

        @pl.when(i < 15)
        def _():
            attn_copy(block).start()

    attn[:, my_col] = attn_stage[me]

    @pl.loop(1, 16)
    def _(i):
        src = (me - i + 16) % 16
        col = pl.ds(pl.multiple_of(src * HD, HD), HD)
        remote(
            attn_stage.at[src], attn.at[:, col], attn_s.at[src], attn_r.at[src], sibling
        ).wait_recv()

    square = jnp.zeros((TOK, 1), F32)
    for n in range(NCH):
        cols = slice(n * CH, (n + 1) * CH)
        wo_copy(n).wait()
        mixed = jnp.dot(attn[...], wo_buf[n % 2], preferred_element_type=F32)
        summed = (hidden[:, cols].astype(F32) + mixed).astype(BF16)
        resid[:, cols] = summed
        wide = summed.astype(F32)
        square = square + jnp.sum(wide * wide, axis=1, keepdims=True)
        if n + 2 < NCH:
            wo_copy(n + 2).start()
    inverse = lax.rsqrt(square * (1.0 / D) + EPS)
    my_rows = pl.ds(pl.multiple_of(z * TOK, TOK), TOK)

    mate = z + 1 - 2 * (z % 2)
    across = 3 - z

    def tok_copy(c, hop):
        owner = mate if hop == 2 else z
        rows = pl.ds(pl.multiple_of(owner * TOK, TOK), TOK)
        block = tok.at[rows, pl.ds(c * CH, CH)]
        return remote(
            block, block, tok_s.at[c, hop], tok_r.at[c, hop],
            peer(x, y, mate if hop == 0 else across, core),
        )

    def tok_arrival(c, hop):
        owner = (mate, across, 3 - mate)[hop]
        rows = pl.ds(pl.multiple_of(owner * TOK, TOK), TOK)
        block = tok.at[rows, pl.ds(c * CH, CH)]
        remote(block, block, tok_s.at[c, hop], tok_r.at[c, hop], sibling).wait_recv()

    for c in range(NCH):
        cols = slice(c * CH, (c + 1) * CH)
        tok[my_rows, cols] = (resid[:, cols].astype(F32) * inverse * moe_gain[:, cols]).astype(BF16)
        tok_copy(c, 0).start()
        tok_copy(c, 1).start()

    @pl.when(jnp.logical_not(kappa))
    def _():
        for n in range(3):
            cross_weight(n).start()

    def row_block(r):
        return pl.ds(pl.multiple_of(r * ROWS, ROWS), ROWS)

    def disp_copy(r, c):
        rows = row_block(r)
        cols = pl.ds(c * CH, CH)
        return remote(
            stage.at[rows, cols], arrive.at[rows, cols], disp_s.at[r, c], disp_r.at[r, c],
            peer((x + pick(OFFSETS, 0, r)) % 4, (y + pick(OFFSETS, 1, r)) % 4, z, core),
        )

    def select_rows(g, c):
        rows = pl.ds(pl.multiple_of(g * 4 * ROWS, 4 * ROWS), 4 * ROWS)
        cols = slice(c * CH, (c + 1) * CH)
        picked = jnp.dot(sel[rows, :], tok[:, cols], preferred_element_type=F32)
        stage[rows, cols] = picked.astype(BF16)

    def not_self(r, action):
        if isinstance(r, int):
            if r != SELF:
                action()
        else:
            pl.when(r != SELF)(action)

    def disp_group(g, act_on):
        for i in range(4):
            def action(r=g * 4 + i):
                for c in range(NCH):
                    act_on(disp_copy(r, c))

            not_self(g * 4 + i, action)

    for c in range(NCH):
        cols = slice(c * CH, (c + 1) * CH)
        tok_arrival(c, 0)
        tok_copy(c, 2).start()
        tok_arrival(c, 1)
        tok_arrival(c, 2)
        select_rows(0, c)
        for i in range(4):
            disp_copy(i, c).start()

    @pl.loop(1, 4)
    def _(g):
        for c in range(NCH):
            select_rows(g, c)
            for i in range(4):
                not_self(g * 4 + i, lambda r=g * 4 + i: disp_copy(r, c).start())

    self_rows = slice(SELF * ROWS, (SELF + 1) * ROWS)
    arrive[self_rows, :] = stage[self_rows, :]

    def near_weight(n):
        @pl.when(kappa)
        def _():
            local_weight(n).wait()

        @pl.when(jnp.logical_not(kappa))
        def _():
            first_weight(n).wait_recv()

    def far_weight(n):
        @pl.when(kappa)
        def _():
            cross_weight(n).wait_recv()
            second_weight(n).start()

        @pl.when(jnp.logical_not(kappa))
        def _():
            second_weight(n).wait_recv()

    for n in range(2):
        near_weight(n)
        far_weight(n)

    @pl.loop(0, 4)
    def _(g):
        disp_group(g, lambda copy: copy.wait_recv())
        rows = pl.ds(pl.multiple_of(g * 4 * ROWS, 4 * ROWS), 4 * ROWS)
        for s in range(2):
            gate = jnp.dot(arrive[rows, :], gate_b[s], preferred_element_type=F32)
            up = jnp.dot(arrive[rows, :], up_b[s], preferred_element_type=F32)
            act[rows, s * FFH : (s + 1) * FFH] = (
                gate * (1.0 / (1.0 + jnp.exp(-gate))) * up
            ).astype(BF16)

    def ret_copy(r, c):
        rows = row_block(r)
        cols = pl.ds(c * CH, CH)
        return remote(
            arrive.at[rows, cols], ret.at[rows, cols], ret_s.at[r, c], ret_r.at[r, c],
            peer((x - pick(OFFSETS, 0, r) + 4) % 4, (y - pick(OFFSETS, 1, r) + 4) % 4, z, core),
        )

    def ret_chunk(c, act_on):
        @pl.loop(0, PLANE)
        def _(r):
            not_self(r, lambda: act_on(ret_copy(r, c)))

    def down_rows(c):
        cols = slice(c * CH, (c + 1) * CH)

        @pl.loop(0, 4)
        def _(g):
            rows = pl.ds(pl.multiple_of(g * 4 * ROWS, 4 * ROWS), 4 * ROWS)
            piece = jnp.dot(act[rows, 0:FFH], down_b[0, :, cols], preferred_element_type=F32)
            piece = piece + jnp.dot(
                act[rows, FFH : 2 * FFH], down_b[1, :, cols], preferred_element_type=F32
            )
            arrive[rows, cols] = piece.astype(BF16)

        ret[self_rows, cols] = arrive[self_rows, cols]

    def part_copy(c, dz):
        target = (z + dz) % 4
        rows = pl.ds(pl.multiple_of(target * TOK, TOK), TOK)
        return remote(
            part_stage.at[c, rows, :], part_in.at[c, dz - 1],
            part_s.at[c, dz - 1], part_r.at[c, dz - 1], peer(x, y, target, core),
        )

    def combine(c):
        cols = slice(c * CH, (c + 1) * CH)

        ret_chunk(c, lambda copy: copy.wait_recv())
        sums = lax.dot_general(
            wsel[...], ret[:, cols], (((0,), (0,)), ((), ())), preferred_element_type=F32
        )
        part_stage[c] = sums.astype(BF16)
        for dz in (1, 3, 2):
            part_copy(c, dz).start()
        part[...] = sums
        return part[my_rows, :]

    def finish(c, own, score):
        cols = slice(c * CH, (c + 1) * CH)
        total = own
        for dz in range(1, 4):
            part_copy(c, dz).wait_recv()
            total = total + part_in[c, dz - 1].astype(F32)
        out = (resid[:, cols].astype(F32) + total).astype(BF16)
        lay[:, cols] = out
        return score + jnp.sum(out.astype(F32) * score_w[:, cols], axis=1, keepdims=True)

    def send_back(c):
        ret_chunk(c, lambda copy: copy.start())

    def sent_back(c):
        ret_chunk(c, lambda copy: copy.wait_send())

    near_weight(2)
    far_weight(2)
    score = jnp.zeros((TOK, 1), F32)
    down_rows(0)
    send_back(0)
    down_rows(1)
    send_back(1)
    down_rows(2)
    sent_back(0)
    send_back(2)
    own_0 = combine(0)
    down_rows(3)
    sent_back(1)
    send_back(3)
    own_1 = combine(1)
    score = finish(0, own_0, score)
    own_2 = combine(2)
    score = finish(1, own_1, score)
    own_3 = combine(3)
    score = finish(2, own_2, score)
    score = finish(3, own_3, score)

    member = (starts <= own_pos) & (ends > own_pos)
    sums = jnp.sum(jnp.where(member, score, 0.0), axis=0, keepdims=True)
    dsum[me, :, 0:DOCS] = jnp.broadcast_to(sums, (8, DOCS))
    dsum[me, :, DOCS:128] = jnp.zeros((8, 128 - DOCS), F32)

    def dsum_copy(target):
        return remote(dsum.at[me], dsum.at[me], dsum_s.at[target], dsum_r.at[me], (req, target))

    @pl.loop(1, 16)
    def _(i):
        dsum_copy((me + i) % 16).start()

    for dz in range(1, 4):
        meta_copy(dz).wait_send()
    for n in range(3):
        @pl.when(kappa)
        def _():
            first_weight(n).wait_send()
            second_weight(n).wait_send()

        @pl.when(jnp.logical_not(kappa))
        def _():
            cross_weight(n).wait_send()

    @pl.loop(1, 16)
    def _(i):
        head_copy((me + i) % 16).wait_send()
        attn_copy((me + i) % 16).wait_send()

    for c in range(NCH):
        for n in range(3):
            tok_copy(c, n).wait_send()
            part_copy(c, n + 1).wait_send()

    @pl.loop(0, 4)
    def _(g):
        disp_group(g, lambda copy: copy.wait_send())

    sent_back(2)
    sent_back(3)

    @pl.loop(1, 16)
    def _(i):
        src = (me - i + 16) % 16
        remote(
            dsum.at[src], dsum.at[src], dsum_s.at[src], dsum_r.at[src], sibling
        ).wait_recv()

    whole = dsum[0]
    for n in range(1, 16):
        whole = whole + dsum[n]
    doc_out[...] = whole[0:1, 0:DOCS] / len_row

    @pl.loop(1, 16)
    def _(i):
        dsum_copy((me + i) % 16).wait_send()


def local(
    hidden_in, qkv, q_gain, k_gain, query_pages, page_table, doc_lengths, doc_query, out_weight,
    moe_gain, routes, route_weight, gate_weight, up_weight, down_weight, score_weight,
):
    half = ROPE_BASE ** (-(np.arange(HD // 2, dtype=np.float32) * 2.0 / HD))
    freq = jnp.asarray(np.concatenate([half, half])[None].astype(np.float32))
    vmem = pl.BlockSpec(memory_space=pltpu.VMEM)
    hbm = pl.BlockSpec(memory_space=pl.ANY)
    dma = pltpu.SemaphoreType.DMA
    call = pl.pallas_call(
        kernel,
        out_shape=(
            jax.ShapeDtypeStruct((TOK, D), BF16),
            jax.ShapeDtypeStruct((1, DOCS), F32),
        ),
        in_specs=[
            vmem, vmem, vmem, vmem, vmem, vmem, vmem, vmem, hbm, vmem, vmem, vmem,
            hbm, hbm, hbm, vmem, vmem,
        ],
        out_specs=(vmem, vmem),
        scratch_shapes=[
            pltpu.VMEM((HEADS, TOK, 3 * HD), BF16),
            pltpu.VMEM((HEADS, TOK, 3 * HD), BF16),
            pltpu.VMEM((TOK, D), BF16),
            pltpu.VMEM((HEADS, TOK, HD), BF16),
            pltpu.VMEM((2, D, CH), BF16),
            pltpu.VMEM((2, D, FFH), BF16),
            pltpu.VMEM((2, D, FFH), BF16),
            pltpu.VMEM((2, FFH, D), BF16),
            pltpu.VMEM((LINE, 16, TOK), F32),
            pltpu.VMEM((LINE * TOK, LINE * TOK), BF16),
            pltpu.VMEM((PLANE, LINE * TOK), F32),
            pltpu.VMEM((PLANE, LINE * TOK), F32),
            pltpu.VMEM((PLANE * ROWS, LINE * TOK), BF16),
            pltpu.VMEM((PLANE * ROWS, LINE * TOK), BF16),
            pltpu.VMEM((TOK, D), BF16),
            pltpu.VMEM((LINE * TOK, D), BF16),
            pltpu.VMEM((PLANE * ROWS, D), BF16),
            pltpu.VMEM((PLANE * ROWS, D), BF16),
            pltpu.VMEM((PLANE * ROWS, 2 * FFH), BF16),
            pltpu.VMEM((PLANE * ROWS, D), BF16),
            pltpu.VMEM((LINE * TOK, CH), F32),
            pltpu.VMEM((NCH, LINE * TOK, CH), BF16),
            pltpu.VMEM((NCH, LINE - 1, TOK, CH), BF16),
            pltpu.VMEM((16, 8, 128), F32),
            dma((16,)), dma((16,)), dma((16,)), dma((16,)), dma((2,)),
            dma((3,)), dma((3,)), dma((3,)), dma((3,)), dma((3,)), dma((3,)), dma((3,)),
            dma((NCH, 3)), dma((NCH, 3)),
            dma((PLANE, NCH)), dma((PLANE, NCH)), dma((PLANE, NCH)), dma((PLANE, NCH)),
            dma((NCH, 3)), dma((NCH, 3)), dma((16,)), dma((16,)),
        ],
        compiler_params=pltpu.CompilerParams(
            collective_id=0, has_side_effects=True, vmem_limit_bytes=60 * 1024 * 1024
        ),
        cost_estimate=pl.CostEstimate(
            flops=26_000_000_000, bytes_accessed=20_000_000, transcendentals=3_000_000
        ),
    )
    return call(
        hidden_in, qkv, q_gain[None], k_gain[None], query_pages[0], page_table, doc_lengths,
        doc_query, out_weight, moe_gain[None], routes, route_weight, gate_weight, up_weight, down_weight,
        score_weight[None], freq,
    )


def solution(mesh):
    rows = P(("req", "exp"), None)
    blocks = P(("req", "exp"), None, None)
    in_specs = (
        rows, rows, P(), P(), P("req", None, None, "exp"), P("req", None), P("req", None),
        P("req", None), P(), P(), rows, rows, blocks, blocks, blocks, P(),
    )
    out_specs = (rows, P("req", None))
    return jax.shard_map(local, mesh=mesh, in_specs=in_specs, out_specs=out_specs, check_vma=False)
```

```python
import functools

import jax
import jax.numpy as jnp
import numpy as np
from jax import lax
from jax.experimental import pallas as pl
from jax.experimental.pallas import tpu as pltpu
from jax.sharding import PartitionSpec as P

D = 2048
HEADS = 16
HD = 128
FFH = 512
TOK = 128
DOCS = 32
NQ = 8
PAGE = 128
CAP = 24
LINE = 4
ROWS = LINE * CAP
PLANE = 16
NCH = 4
CH = D // NCH
NWO = 4
WO = D // NWO
EPS = 1e-06
ROPE_BASE = 50000.0
NEG = -1e30

OFFSETS = (
    (1, 2), (3, 2), (2, 1), (2, 3),
    (1, 3), (3, 1), (2, 0), (0, 2),
    (0, 0), (2, 2), (1, 1), (3, 3),
    (1, 0), (3, 0), (0, 1), (0, 3),
)
SELF = OFFSETS.index((0, 0))
OTHERS_THEN_SELF = OFFSETS[:SELF] + OFFSETS[SELF + 1 :] + OFFSETS[SELF : SELF + 1]

F32 = jnp.float32
BF16 = jnp.bfloat16
MESH = pl.DeviceIdType.MESH


def iota(shape, dim):
    return lax.broadcasted_iota(jnp.int32, shape, dim)


def iota_f(shape, dim):
    return iota(shape, dim).astype(F32)


def pick(table, axis, index):
    if isinstance(index, int):
        return table[index][axis]
    value = table[-1][axis]
    for n in range(len(table) - 1):
        value = jnp.where(index == n, table[n][axis], value)
    return value


def kernel(
    hidden, qkv, q_gain, k_gain, pages, page_table, doc_len, doc_query, w_out, moe_gain, routes, route_w,
    gate_w, up_w, down_w, score_w, freq,
    lay, doc_out,
    head_stage, head_all, attn, attn_stage, wo_buf, gate_b, up_b, down_b, meta_all, tri, rank,
    wrow, sel, wsel, resid, tok, stage, arrive, act, ret, part, part_stage, part_in, dsum,
    head_s, head_r, attn_s, attn_r, wo_sem, meta_s, meta_r, loc_sem, wa_s, wa_r, wb_s, wb_r,
    tok_s, tok_r, disp_s, disp_r, ret_s, ret_r, part_s, part_r, dsum_s, dsum_r,
):
    req = lax.axis_index("req")
    me = lax.axis_index("exp")
    y, core = req // 2, req % 2
    x, z = me // 4, me % 4
    kappa = core == z % 2

    def peer(px, py, pz, pc):
        return (2 * py + pc, 4 * px + pz)

    sibling = (2 * y + (1 - core), me)
    partner = (req, 4 * x + (z + 1 - 2 * (z % 2)))

    barrier = pltpu.get_barrier_semaphore()

    @pl.loop(1, 16)
    def _(i):
        pl.semaphore_signal(barrier, 1, device_id=(req, (me + i) % 16), device_id_type=MESH)

    @pl.loop(1, 4)
    def _(dy):
        @pl.loop(0, 4)
        def _(dx):
            pl.semaphore_signal(
                barrier, 1, device_id=peer((x + dx) % 4, (y + dy) % 4, z, core), device_id_type=MESH
            )

    pl.semaphore_signal(barrier, 1, device_id=sibling, device_id_type=MESH)
    pl.semaphore_wait(barrier, 28)

    def remote(src, dst, send, recv, device):
        return pltpu.make_async_remote_copy(
            src_ref=src, dst_ref=dst, send_sem=send, recv_sem=recv, device_id=device, device_id_type=MESH
        )

    weights = ((gate_w, gate_b), (up_w, up_b), (down_w, down_b))

    def local_weight(n):
        return pltpu.make_async_copy(weights[n][0].at[0], weights[n][1].at[0], loc_sem.at[n])

    def first_weight(n):
        return remote(
            weights[n][0].at[0], weights[n][1].at[0], wa_s.at[n], wa_r.at[n], sibling
        )

    def cross_weight(n):
        return remote(
            weights[n][0].at[0], weights[n][1].at[1], wa_s.at[n], wb_r.at[n], partner
        )

    def second_weight(n):
        return remote(
            weights[n][1].at[1], weights[n][1].at[1], wb_s.at[n], wb_r.at[n], sibling
        )

    def meta_copy(dz):
        return remote(
            meta_all.at[z], meta_all.at[z], meta_s.at[dz - 1], meta_r.at[dz - 1],
            peer(x, y, (z + dz) % 4, core),
        )

    identity = jnp.where(iota((TOK, TOK), 0) == iota((TOK, TOK), 1), 1.0, 0.0).astype(BF16)

    def turned(values):
        return lax.dot_general(
            values.astype(BF16), identity, (((0,), (0,)), ((), ())), preferred_element_type=F32
        )

    meta_all[z, 0:8, :] = turned(routes[...].astype(F32))
    meta_all[z, 8:16, :] = turned(route_w[...])
    for dz in range(1, 4):
        meta_copy(dz).start()

    def wo_copy(n):
        return pltpu.make_async_copy(
            w_out.at[:, pl.ds(n * WO, WO)], wo_buf.at[n % 3], wo_sem.at[n % 3]
        )

    for n in range(3):
        wo_copy(n).start()

    len_row = doc_len[...].astype(F32)
    eye = iota((DOCS, DOCS), 0) == iota((DOCS, DOCS), 1)
    len_col = jnp.sum(jnp.where(eye, len_row, 0.0), axis=1, keepdims=True)
    upto = iota((DOCS, DOCS), 0) <= iota((DOCS, DOCS), 1)
    ends = jnp.sum(jnp.where(upto, len_col, 0.0), axis=0, keepdims=True)
    starts = ends - len_row
    eye_q = iota((NQ, NQ), 0) == iota((NQ, NQ), 1)
    page_col = jnp.sum(
        jnp.where(eye_q, page_table[...].astype(F32), 0.0), axis=1, keepdims=True
    )
    page_row = jnp.sum(
        jnp.where(doc_query[...] == iota((NQ, DOCS), 0), page_col, 0.0), axis=0, keepdims=True
    )

    def positions(block):
        return (block * TOK).astype(F32) + iota_f((TOK, 1), 0)

    own_pos = positions(me)
    own_start = jnp.max(jnp.where(starts <= own_pos, starts, 0.0), axis=1, keepdims=True)
    angles = (PAGE + own_pos - own_start) * freq[...]
    cosine = jnp.cos(angles)
    sine = jnp.sin(angles)
    sine = jnp.where(iota((TOK, HD), 1) < HD // 2, -sine, sine)

    def norm_rope(values, gain):
        values = values.astype(F32)
        mean_sq = jnp.mean(values * values, axis=-1, keepdims=True)
        values = values * lax.rsqrt(mean_sq + EPS) * gain[...]
        return (values * cosine + pltpu.roll(values, HD // 2, 1) * sine).astype(BF16)

    def head_copy(head):
        return remote(
            head_stage.at[head], head_all.at[me], head_s.at[head], head_r.at[me], (req, head)
        )

    def plane_member(i):
        return 4 * ((x + pick(OTHERS_THEN_SELF, 0, i)) % 4) + (z + pick(OTHERS_THEN_SELF, 1, i)) % 4

    @pl.loop(0, 16)
    def _(i):
        head = plane_member(i)
        col = pl.multiple_of(head * HD, HD)
        head_stage[head, :, 0:HD] = norm_rope(qkv[:, pl.ds(col, HD)], q_gain)
        head_stage[head, :, HD : 2 * HD] = norm_rope(qkv[:, pl.ds(D + col, HD)], k_gain)
        head_stage[head, :, 2 * HD : 3 * HD] = qkv[:, pl.ds(2 * D + col, HD)]

        @pl.when(i < 15)
        def _():
            head_copy(head).start()

    head_all[me] = head_stage[me]

    @pl.when(kappa)
    def _():
        for n in range(3):
            local_weight(n).start()
            first_weight(n).start()

    for dz in range(1, 4):
        src = (z - dz + 4) % 4
        remote(
            meta_all.at[src], meta_all.at[src], meta_s.at[dz - 1], meta_r.at[dz - 1], sibling
        ).wait_recv()
    slot = iota((PLANE, 1), 0)
    to_x = (pick(OFFSETS, 0, slot) + x) % 4
    to_y = (pick(OFFSETS, 1, slot) + y) % 4
    expert = ((2 * to_y + z % 2) * 8 + 2 * to_x + z // 2).astype(F32)
    for j in range(LINE):
        mask = jnp.zeros((PLANE, TOK), F32)
        weight = jnp.zeros((PLANE, TOK), F32)
        for n in range(8):
            hit = meta_all[j, n : n + 1, :] == expert
            mask = jnp.where(hit, 1.0, mask)
            weight = jnp.where(hit, meta_all[j, 8 + n : 9 + n, :], weight)
        rank[:, j * TOK : (j + 1) * TOK] = mask
        wrow[:, j * TOK : (j + 1) * TOK] = weight
    tri[...] = jnp.where(
        iota((LINE * TOK, LINE * TOK), 0) < iota((LINE * TOK, LINE * TOK), 1), 1.0, 0.0
    ).astype(BF16)
    mask = rank[...]
    prior = jnp.dot(mask.astype(BF16), tri[...], preferred_element_type=F32)
    rank[...] = jnp.where(mask > 0.0, prior, -1.0)

    @pl.loop(0, PLANE)
    def _(r):
        hit = rank[pl.ds(r, 1), :] == iota_f((ROWS, LINE * TOK), 0)
        rows = pl.ds(pl.multiple_of(r * ROWS, ROWS), ROWS)
        sel[rows, :] = jnp.where(hit, 1.0, 0.0).astype(BF16)
        wsel[rows, :] = jnp.where(hit, wrow[pl.ds(r, 1), :], 0.0).astype(BF16)

    @pl.loop(1, 16)
    def _(i):
        src = (me - i + 16) % 16
        remote(
            head_stage.at[src], head_all.at[src], head_s.at[src], head_r.at[src], sibling
        ).wait_recv()

    page_keys = pages[:, :, 0:HD].reshape(NQ * PAGE, HD)
    page_values = pages[:, :, HD : 2 * HD].reshape(NQ * PAGE, HD)
    my_col = pl.ds(pl.multiple_of(me * HD, HD), HD)

    def attn_copy(block):
        return remote(
            attn_stage.at[block], attn.at[:, my_col], attn_s.at[block], attn_r.at[me], (req, block)
        )

    contract_last = (((1,), (1,)), ((), ()))

    @pl.loop(0, 16)
    def _(i):
        block = plane_member(i)
        first = jnp.clip(block - 1, 0, 13)
        query = head_all[block, :, 0:HD]
        keys = head_all[pl.ds(first, 3), :, HD : 2 * HD].reshape(3 * TOK, HD)
        values = head_all[pl.ds(first, 3), :, 2 * HD : 3 * HD].reshape(3 * TOK, HD)
        pos = positions(block)
        began = starts <= pos
        left = ends > pos
        start = jnp.max(jnp.where(began, starts, 0.0), axis=1, keepdims=True)
        end = jnp.min(jnp.where(left, ends, 4096.0), axis=1, keepdims=True)
        page = jnp.sum(jnp.where(began & left, page_row, 0.0), axis=1, keepdims=True)
        scale = HD**-0.5
        near = lax.dot_general(query, keys, contract_last, preferred_element_type=F32) * scale
        paged = lax.dot_general(query, page_keys, contract_last, preferred_element_type=F32)
        own = paged[:, 0:PAGE]
        for n in range(1, NQ):
            own = jnp.where(page == float(n), paged[:, n * PAGE : (n + 1) * PAGE], own)
        own = own * scale
        key_pos = (first * TOK).astype(F32) + iota_f((TOK, 3 * TOK), 1)
        visible = (key_pos >= start) & (key_pos < end)
        near = jnp.where(visible, near, NEG)
        top = jnp.maximum(
            jnp.max(near, axis=1, keepdims=True), jnp.max(own, axis=1, keepdims=True)
        )
        near = jnp.where(visible, jnp.exp(near - top), 0.0)
        own = jnp.exp(own - top)
        total = jnp.sum(near, axis=1, keepdims=True) + jnp.sum(own, axis=1, keepdims=True)
        spread = jnp.concatenate(
            [jnp.where(page == float(n), own, 0.0).astype(BF16) for n in range(NQ)], axis=1
        )
        weighted = jnp.dot(near.astype(BF16), values, preferred_element_type=F32)
        weighted = weighted + jnp.dot(spread, page_values, preferred_element_type=F32)
        attn_stage[block] = (weighted / total).astype(BF16)

        @pl.when(i < 15)
        def _():
            attn_copy(block).start()

    attn[:, my_col] = attn_stage[me]

    @pl.loop(1, 16)
    def _(i):
        src = (me - i + 16) % 16
        col = pl.ds(pl.multiple_of(src * HD, HD), HD)
        remote(
            attn_stage.at[src], attn.at[:, col], attn_s.at[src], attn_r.at[src], sibling
        ).wait_recv()

    square = jnp.zeros((TOK, 1), F32)
    for n in range(NWO):
        cols = slice(n * WO, (n + 1) * WO)
        wo_copy(n).wait()
        mixed = jnp.dot(attn[...], wo_buf[n % 3], preferred_element_type=F32)
        summed = (hidden[:, cols].astype(F32) + mixed).astype(BF16)
        resid[:, cols] = summed
        wide = summed.astype(F32)
        square = square + jnp.sum(wide * wide, axis=1, keepdims=True)
        if n + 3 < NWO:
            wo_copy(n + 3).start()
    inverse = lax.rsqrt(square * (1.0 / D) + EPS)
    my_rows = pl.ds(pl.multiple_of(z * TOK, TOK), TOK)

    mate = z + 1 - 2 * (z % 2)
    across = 3 - z

    def tok_copy(c, hop):
        owner = mate if hop == 2 and c > 0 else z
        rows = pl.ds(pl.multiple_of(owner * TOK, TOK), TOK)
        block = tok.at[rows, pl.ds(c * CH, CH)]
        return remote(
            block, block, tok_s.at[c, hop], tok_r.at[c, hop],
            peer(x, y, (mate, across, across if c > 0 else (z + 2) % 4)[hop], core),
        )

    def tok_arrival(c, hop):
        owner = (mate, across, 3 - mate)[hop]
        rows = pl.ds(pl.multiple_of(owner * TOK, TOK), TOK)
        block = tok.at[rows, pl.ds(c * CH, CH)]
        remote(block, block, tok_s.at[c, hop], tok_r.at[c, hop], sibling).wait_recv()

    for c in range(NCH):
        cols = slice(c * CH, (c + 1) * CH)
        tok[my_rows, cols] = (resid[:, cols].astype(F32) * inverse * moe_gain[:, cols]).astype(BF16)
        for hop in range(3 if c == 0 else 2):
            tok_copy(c, hop).start()

    @pl.when(jnp.logical_not(kappa))
    def _():
        for n in range(3):
            cross_weight(n).start()

    def row_block(r):
        return pl.ds(pl.multiple_of(r * ROWS, ROWS), ROWS)

    def disp_copy(r, c):
        rows = row_block(r)
        cols = pl.ds(c * CH, CH)
        return remote(
            stage.at[rows, cols], arrive.at[rows, cols], disp_s.at[r, c], disp_r.at[r, c],
            peer((x + pick(OFFSETS, 0, r)) % 4, (y + pick(OFFSETS, 1, r)) % 4, z, core),
        )

    def select_rows(g, c):
        rows = pl.ds(pl.multiple_of(g * 4 * ROWS, 4 * ROWS), 4 * ROWS)
        cols = slice(c * CH, (c + 1) * CH)
        picked = jnp.dot(sel[rows, :], tok[:, cols], preferred_element_type=F32)
        stage[rows, cols] = picked.astype(BF16)

    def not_self(r, action):
        if isinstance(r, int):
            if r != SELF:
                action()
        else:
            pl.when(r != SELF)(action)

    def disp_group(g, act_on):
        for i in range(4):
            def action(r=g * 4 + i):
                for c in range(NCH):
                    act_on(disp_copy(r, c))

            not_self(g * 4 + i, action)

    for c in range(NCH):
        cols = slice(c * CH, (c + 1) * CH)
        tok_arrival(c, 0)
        if c > 0:
            tok_copy(c, 2).start()
        tok_arrival(c, 1)
        tok_arrival(c, 2)
        select_rows(0, c)
        for i in range(4):
            disp_copy(i, c).start()

    @pl.loop(1, 4)
    def _(g):
        for c in range(NCH):
            select_rows(g, c)
            for i in range(4):
                not_self(g * 4 + i, lambda r=g * 4 + i: disp_copy(r, c).start())

    self_rows = slice(SELF * ROWS, (SELF + 1) * ROWS)
    arrive[self_rows, :] = stage[self_rows, :]

    def near_weight(n):
        @pl.when(kappa)
        def _():
            local_weight(n).wait()

        @pl.when(jnp.logical_not(kappa))
        def _():
            first_weight(n).wait_recv()

    def far_weight(n):
        @pl.when(kappa)
        def _():
            cross_weight(n).wait_recv()
            second_weight(n).start()

        @pl.when(jnp.logical_not(kappa))
        def _():
            second_weight(n).wait_recv()

    for n in range(2):
        near_weight(n)
        far_weight(n)

    @pl.loop(0, 4)
    def _(g):
        disp_group(g, lambda copy: copy.wait_recv())
        rows = pl.ds(pl.multiple_of(g * 4 * ROWS, 4 * ROWS), 4 * ROWS)
        for s in range(2):
            gate = jnp.dot(arrive[rows, :], gate_b[s], preferred_element_type=F32)
            up = jnp.dot(arrive[rows, :], up_b[s], preferred_element_type=F32)
            act[rows, s * FFH : (s + 1) * FFH] = (
                gate * (1.0 / (1.0 + jnp.exp(-gate))) * up
            ).astype(BF16)

    def ret_copy(r, c):
        rows = row_block(r)
        cols = pl.ds(c * CH, CH)
        return remote(
            arrive.at[rows, cols], ret.at[rows, cols], ret_s.at[r, c], ret_r.at[r, c],
            peer((x - pick(OFFSETS, 0, r) + 4) % 4, (y - pick(OFFSETS, 1, r) + 4) % 4, z, core),
        )

    def ret_chunk(c, act_on):
        @pl.loop(0, PLANE)
        def _(r):
            not_self(r, lambda: act_on(ret_copy(r, c)))

    def down_rows(c):
        cols = slice(c * CH, (c + 1) * CH)

        @pl.loop(0, 4)
        def _(g):
            rows = pl.ds(pl.multiple_of(g * 4 * ROWS, 4 * ROWS), 4 * ROWS)
            piece = jnp.dot(act[rows, 0:FFH], down_b[0, :, cols], preferred_element_type=F32)
            piece = piece + jnp.dot(
                act[rows, FFH : 2 * FFH], down_b[1, :, cols], preferred_element_type=F32
            )
            arrive[rows, cols] = piece.astype(BF16)

        ret[self_rows, cols] = arrive[self_rows, cols]

    def part_copy(c, dz):
        target = (z + dz) % 4
        rows = pl.ds(pl.multiple_of(target * TOK, TOK), TOK)
        return remote(
            part_stage.at[c, rows, :], part_in.at[c, dz - 1],
            part_s.at[c, dz - 1], part_r.at[c, dz - 1], peer(x, y, target, core),
        )

    def combine(c):
        cols = slice(c * CH, (c + 1) * CH)

        ret_chunk(c, lambda copy: copy.wait_recv())
        sums = lax.dot_general(
            wsel[...], ret[:, cols], (((0,), (0,)), ((), ())), preferred_element_type=F32
        )
        part_stage[c] = sums.astype(BF16)
        for dz in (1, 3, 2):
            part_copy(c, dz).start()
        part[...] = sums
        return part[my_rows, :]

    def finish(c, own, score):
        cols = slice(c * CH, (c + 1) * CH)
        total = own
        for dz in range(1, 4):
            part_copy(c, dz).wait_recv()
            total = total + part_in[c, dz - 1].astype(F32)
        out = (resid[:, cols].astype(F32) + total).astype(BF16)
        lay[:, cols] = out
        return score + jnp.sum(out.astype(F32) * score_w[:, cols], axis=1, keepdims=True)

    def send_back(c):
        ret_chunk(c, lambda copy: copy.start())

    def sent_back(c):
        ret_chunk(c, lambda copy: copy.wait_send())

    near_weight(2)
    far_weight(2)
    score = jnp.zeros((TOK, 1), F32)
    own = {}
    for step in range(NCH + 3):
        if step < NCH:
            down_rows(step)
            if step >= 2:
                sent_back(step - 2)
            send_back(step)
        if 2 <= step < NCH + 2:
            own[step - 2] = combine(step - 2)
        if step >= 3:
            score = finish(step - 3, own.pop(step - 3), score)

    member = (starts <= own_pos) & (ends > own_pos)
    sums = jnp.sum(jnp.where(member, score, 0.0), axis=0, keepdims=True)
    dsum[me, :, 0:DOCS] = jnp.broadcast_to(sums, (8, DOCS))
    dsum[me, :, DOCS:128] = jnp.zeros((8, 128 - DOCS), F32)

    def dsum_copy(target):
        return remote(dsum.at[me], dsum.at[me], dsum_s.at[target], dsum_r.at[me], (req, target))

    @pl.loop(1, 16)
    def _(i):
        dsum_copy((me + i) % 16).start()

    for dz in range(1, 4):
        meta_copy(dz).wait_send()
    for n in range(3):
        @pl.when(kappa)
        def _():
            first_weight(n).wait_send()
            second_weight(n).wait_send()

        @pl.when(jnp.logical_not(kappa))
        def _():
            cross_weight(n).wait_send()

    @pl.loop(1, 16)
    def _(i):
        head_copy((me + i) % 16).wait_send()
        attn_copy((me + i) % 16).wait_send()

    for c in range(NCH):
        for n in range(3):
            tok_copy(c, n).wait_send()
            part_copy(c, n + 1).wait_send()

    @pl.loop(0, 4)
    def _(g):
        disp_group(g, lambda copy: copy.wait_send())

    sent_back(NCH - 2)
    sent_back(NCH - 1)

    @pl.loop(1, 16)
    def _(i):
        src = (me - i + 16) % 16
        remote(
            dsum.at[src], dsum.at[src], dsum_s.at[src], dsum_r.at[src], sibling
        ).wait_recv()

    whole = dsum[0]
    for n in range(1, 16):
        whole = whole + dsum[n]
    doc_out[...] = whole[0:1, 0:DOCS] / len_row

    @pl.loop(1, 16)
    def _(i):
        dsum_copy((me + i) % 16).wait_send()


def local(
    hidden_in, qkv, q_gain, k_gain, query_pages, page_table, doc_lengths, doc_query, out_weight,
    moe_gain, routes, route_weight, gate_weight, up_weight, down_weight, score_weight,
):
    half = ROPE_BASE ** (-(np.arange(HD // 2, dtype=np.float32) * 2.0 / HD))
    freq = jnp.asarray(np.concatenate([half, half])[None].astype(np.float32))
    vmem = pl.BlockSpec(memory_space=pltpu.VMEM)
    hbm = pl.BlockSpec(memory_space=pl.ANY)
    dma = pltpu.SemaphoreType.DMA
    call = pl.pallas_call(
        kernel,
        out_shape=(
            jax.ShapeDtypeStruct((TOK, D), BF16),
            jax.ShapeDtypeStruct((1, DOCS), F32),
        ),
        in_specs=[
            vmem, vmem, vmem, vmem, vmem, vmem, vmem, vmem, hbm, vmem, vmem, vmem,
            hbm, hbm, hbm, vmem, vmem,
        ],
        out_specs=(vmem, vmem),
        scratch_shapes=[
            pltpu.VMEM((HEADS, TOK, 3 * HD), BF16),
            pltpu.VMEM((HEADS, TOK, 3 * HD), BF16),
            pltpu.VMEM((TOK, D), BF16),
            pltpu.VMEM((HEADS, TOK, HD), BF16),
            pltpu.VMEM((3, D, WO), BF16),
            pltpu.VMEM((2, D, FFH), BF16),
            pltpu.VMEM((2, D, FFH), BF16),
            pltpu.VMEM((2, FFH, D), BF16),
            pltpu.VMEM((LINE, 16, TOK), F32),
            pltpu.VMEM((LINE * TOK, LINE * TOK), BF16),
            pltpu.VMEM((PLANE, LINE * TOK), F32),
            pltpu.VMEM((PLANE, LINE * TOK), F32),
            pltpu.VMEM((PLANE * ROWS, LINE * TOK), BF16),
            pltpu.VMEM((PLANE * ROWS, LINE * TOK), BF16),
            pltpu.VMEM((TOK, D), BF16),
            pltpu.VMEM((LINE * TOK, D), BF16),
            pltpu.VMEM((PLANE * ROWS, D), BF16),
            pltpu.VMEM((PLANE * ROWS, D), BF16),
            pltpu.VMEM((PLANE * ROWS, 2 * FFH), BF16),
            pltpu.VMEM((PLANE * ROWS, D), BF16),
            pltpu.VMEM((LINE * TOK, CH), F32),
            pltpu.VMEM((NCH, LINE * TOK, CH), BF16),
            pltpu.VMEM((NCH, LINE - 1, TOK, CH), BF16),
            pltpu.VMEM((16, 8, 128), F32),
            dma((16,)), dma((16,)), dma((16,)), dma((16,)), dma((3,)),
            dma((3,)), dma((3,)), dma((3,)), dma((3,)), dma((3,)), dma((3,)), dma((3,)),
            dma((NCH, 3)), dma((NCH, 3)),
            dma((PLANE, NCH)), dma((PLANE, NCH)), dma((PLANE, NCH)), dma((PLANE, NCH)),
            dma((NCH, 3)), dma((NCH, 3)), dma((16,)), dma((16,)),
        ],
        compiler_params=pltpu.CompilerParams(
            collective_id=0, has_side_effects=True, vmem_limit_bytes=60 * 1024 * 1024
        ),
        cost_estimate=pl.CostEstimate(
            flops=26_000_000_000, bytes_accessed=20_000_000, transcendentals=3_000_000
        ),
    )
    return call(
        hidden_in, qkv, q_gain[None], k_gain[None], query_pages[0], page_table, doc_lengths,
        doc_query, out_weight, moe_gain[None], routes, route_weight, gate_weight, up_weight, down_weight,
        score_weight[None], freq,
    )


def solution(mesh):
    rows = P(("req", "exp"), None)
    blocks = P(("req", "exp"), None, None)
    in_specs = (
        rows, rows, P(), P(), P("req", None, None, "exp"), P("req", None), P("req", None),
        P("req", None), P(), P(), rows, rows, blocks, blocks, blocks, P(),
    )
    out_specs = (rows, P("req", None))
    return jax.shard_map(local, mesh=mesh, in_specs=in_specs, out_specs=out_specs, check_vma=False)
```

```python
import functools

import jax
import jax.numpy as jnp
import numpy as np
from jax import lax
from jax.experimental import pallas as pl
from jax.experimental.pallas import tpu as pltpu
from jax.sharding import PartitionSpec as P

D = 2048
HEADS = 16
HD = 128
FFH = 512
TOK = 128
DOCS = 32
NQ = 8
PAGE = 128
CAP = 24
LINE = 4
ROWS = LINE * CAP
PLANE = 16
NCH = 4
CH = D // NCH
NWO = 4
WO = D // NWO
EPS = 1e-06
ROPE_BASE = 50000.0
NEG = -1e30

OFFSETS = (
    (1, 2), (3, 2), (2, 1), (2, 3),
    (1, 3), (3, 1), (2, 0), (0, 2),
    (0, 0), (2, 2), (1, 1), (3, 3),
    (1, 0), (3, 0), (0, 1), (0, 3),
)
SELF = OFFSETS.index((0, 0))
OTHERS_THEN_SELF = OFFSETS[:SELF] + OFFSETS[SELF + 1 :] + OFFSETS[SELF : SELF + 1]

F32 = jnp.float32
BF16 = jnp.bfloat16
MESH = pl.DeviceIdType.MESH


def iota(shape, dim):
    return lax.broadcasted_iota(jnp.int32, shape, dim)


def iota_f(shape, dim):
    return iota(shape, dim).astype(F32)


def pick(table, axis, index):
    if isinstance(index, int):
        return table[index][axis]
    value = table[-1][axis]
    for n in range(len(table) - 1):
        value = jnp.where(index == n, table[n][axis], value)
    return value


def kernel(
    hidden, qkv, q_gain, k_gain, pages, page_table, doc_len, doc_query, w_out, moe_gain, routes, route_w,
    gate_w, up_w, down_w, score_w, freq,
    lay, doc_out,
    head_stage, head_all, attn, attn_stage, wo_buf, gate_b, up_b, down_b, meta_all, tri, rank,
    wrow, sel, wsel, resid, tok, stage, arrive, act, ret, part, part_stage, part_in, dsum,
    head_s, head_r, attn_s, attn_r, wo_sem, meta_s, meta_r, loc_sem, wa_s, wa_r, wb_s, wb_r,
    tok_s, tok_r, disp_s, disp_r, ret_s, ret_r, part_s, part_r, dsum_s, dsum_r,
):
    req = lax.axis_index("req")
    me = lax.axis_index("exp")
    y, core = req // 2, req % 2
    x, z = me // 4, me % 4
    kappa = core == z % 2

    def peer(px, py, pz, pc):
        return (2 * py + pc, 4 * px + pz)

    sibling = (2 * y + (1 - core), me)
    partner = (req, 4 * x + (z + 1 - 2 * (z % 2)))

    barrier = pltpu.get_barrier_semaphore()

    @pl.loop(1, 16)
    def _(i):
        pl.semaphore_signal(barrier, 1, device_id=(req, (me + i) % 16), device_id_type=MESH)

    @pl.loop(1, 4)
    def _(dy):
        @pl.loop(0, 4)
        def _(dx):
            pl.semaphore_signal(
                barrier, 1, device_id=peer((x + dx) % 4, (y + dy) % 4, z, core), device_id_type=MESH
            )

    pl.semaphore_signal(barrier, 1, device_id=sibling, device_id_type=MESH)
    pl.semaphore_wait(barrier, 28)

    def remote(src, dst, send, recv, device):
        return pltpu.make_async_remote_copy(
            src_ref=src, dst_ref=dst, send_sem=send, recv_sem=recv, device_id=device, device_id_type=MESH
        )

    weights = ((gate_w, gate_b), (up_w, up_b), (down_w, down_b))

    def local_weight(n):
        return pltpu.make_async_copy(weights[n][0].at[0], weights[n][1].at[0], loc_sem.at[n])

    def first_weight(n):
        return remote(
            weights[n][0].at[0], weights[n][1].at[0], wa_s.at[n], wa_r.at[n], sibling
        )

    def cross_weight(n):
        return remote(
            weights[n][0].at[0], weights[n][1].at[1], wa_s.at[n], wb_r.at[n], partner
        )

    def second_weight(n):
        return remote(
            weights[n][1].at[1], weights[n][1].at[1], wb_s.at[n], wb_r.at[n], sibling
        )

    def meta_copy(dz):
        return remote(
            meta_all.at[z], meta_all.at[z], meta_s.at[dz - 1], meta_r.at[dz - 1],
            peer(x, y, (z + dz) % 4, core),
        )

    identity = jnp.where(iota((TOK, TOK), 0) == iota((TOK, TOK), 1), 1.0, 0.0).astype(BF16)

    def turned(values):
        return lax.dot_general(
            values.astype(BF16), identity, (((0,), (0,)), ((), ())), preferred_element_type=F32
        )

    meta_all[z, 0:8, :] = turned(routes[...].astype(F32))
    meta_all[z, 8:16, :] = turned(route_w[...])
    for dz in range(1, 4):
        meta_copy(dz).start()

    def wo_copy(n):
        return pltpu.make_async_copy(
            w_out.at[:, pl.ds(n * WO, WO)], wo_buf.at[n % 3], wo_sem.at[n % 3]
        )

    for n in range(3):
        wo_copy(n).start()

    len_row = doc_len[...].astype(F32)
    eye = iota((DOCS, DOCS), 0) == iota((DOCS, DOCS), 1)
    len_col = jnp.sum(jnp.where(eye, len_row, 0.0), axis=1, keepdims=True)
    upto = iota((DOCS, DOCS), 0) <= iota((DOCS, DOCS), 1)
    ends = jnp.sum(jnp.where(upto, len_col, 0.0), axis=0, keepdims=True)
    starts = ends - len_row
    eye_q = iota((NQ, NQ), 0) == iota((NQ, NQ), 1)
    page_col = jnp.sum(
        jnp.where(eye_q, page_table[...].astype(F32), 0.0), axis=1, keepdims=True
    )
    page_row = jnp.sum(
        jnp.where(doc_query[...] == iota((NQ, DOCS), 0), page_col, 0.0), axis=0, keepdims=True
    )

    def positions(block):
        return (block * TOK).astype(F32) + iota_f((TOK, 1), 0)

    own_pos = positions(me)
    own_start = jnp.max(jnp.where(starts <= own_pos, starts, 0.0), axis=1, keepdims=True)
    angles = (PAGE + own_pos - own_start) * freq[...]
    cosine = jnp.cos(angles)
    sine = jnp.sin(angles)
    sine = jnp.where(iota((TOK, HD), 1) < HD // 2, -sine, sine)

    def norm_rope(values, gain):
        values = values.astype(F32)
        mean_sq = jnp.mean(values * values, axis=-1, keepdims=True)
        values = values * lax.rsqrt(mean_sq + EPS) * gain[...]
        return (values * cosine + pltpu.roll(values, HD // 2, 1) * sine).astype(BF16)

    def head_copy(head):
        return remote(
            head_stage.at[head], head_all.at[me], head_s.at[head], head_r.at[me], (req, head)
        )

    def plane_member(i):
        return 4 * ((x + pick(OTHERS_THEN_SELF, 0, i)) % 4) + (z + pick(OTHERS_THEN_SELF, 1, i)) % 4

    @pl.loop(0, 16)
    def _(i):
        head = plane_member(i)
        col = pl.multiple_of(head * HD, HD)
        head_stage[head, :, 0:HD] = norm_rope(qkv[:, pl.ds(col, HD)], q_gain)
        head_stage[head, :, HD : 2 * HD] = norm_rope(qkv[:, pl.ds(D + col, HD)], k_gain)
        head_stage[head, :, 2 * HD : 3 * HD] = qkv[:, pl.ds(2 * D + col, HD)]

        @pl.when(i < 15)
        def _():
            head_copy(head).start()

    head_all[me] = head_stage[me]

    @pl.when(kappa)
    def _():
        for n in range(3):
            local_weight(n).start()
            first_weight(n).start()

    for dz in range(1, 4):
        src = (z - dz + 4) % 4
        remote(
            meta_all.at[src], meta_all.at[src], meta_s.at[dz - 1], meta_r.at[dz - 1], sibling
        ).wait_recv()
    slot = iota((PLANE, 1), 0)
    to_x = (pick(OFFSETS, 0, slot) + x) % 4
    to_y = (pick(OFFSETS, 1, slot) + y) % 4
    expert = ((2 * to_y + z % 2) * 8 + 2 * to_x + z // 2).astype(F32)
    for j in range(LINE):
        mask = jnp.zeros((PLANE, TOK), F32)
        weight = jnp.zeros((PLANE, TOK), F32)
        for n in range(8):
            hit = meta_all[j, n : n + 1, :] == expert
            mask = jnp.where(hit, 1.0, mask)
            weight = jnp.where(hit, meta_all[j, 8 + n : 9 + n, :], weight)
        rank[:, j * TOK : (j + 1) * TOK] = mask
        wrow[:, j * TOK : (j + 1) * TOK] = weight
    tri[...] = jnp.where(
        iota((LINE * TOK, LINE * TOK), 0) < iota((LINE * TOK, LINE * TOK), 1), 1.0, 0.0
    ).astype(BF16)
    mask = rank[...]
    prior = jnp.dot(mask.astype(BF16), tri[...], preferred_element_type=F32)
    rank[...] = jnp.where(mask > 0.0, prior, -1.0)

    @pl.loop(0, PLANE)
    def _(r):
        hit = rank[pl.ds(r, 1), :] == iota_f((ROWS, LINE * TOK), 0)
        rows = pl.ds(pl.multiple_of(r * ROWS, ROWS), ROWS)
        sel[rows, :] = jnp.where(hit, 1.0, 0.0).astype(BF16)
        wsel[rows, :] = jnp.where(hit, wrow[pl.ds(r, 1), :], 0.0).astype(BF16)

    @pl.loop(1, 16)
    def _(i):
        src = (me - i + 16) % 16
        remote(
            head_stage.at[src], head_all.at[src], head_s.at[src], head_r.at[src], sibling
        ).wait_recv()

    page_keys = pages[:, :, 0:HD].reshape(NQ * PAGE, HD)
    page_values = pages[:, :, HD : 2 * HD].reshape(NQ * PAGE, HD)
    my_col = pl.ds(pl.multiple_of(me * HD, HD), HD)

    def attn_copy(block):
        return remote(
            attn_stage.at[block], attn.at[:, my_col], attn_s.at[block], attn_r.at[me], (req, block)
        )

    contract_last = (((1,), (1,)), ((), ()))

    @pl.loop(0, 16)
    def _(i):
        block = plane_member(i)
        first = jnp.clip(block - 1, 0, 13)
        query = head_all[block, :, 0:HD]
        keys = head_all[pl.ds(first, 3), :, HD : 2 * HD].reshape(3 * TOK, HD)
        values = head_all[pl.ds(first, 3), :, 2 * HD : 3 * HD].reshape(3 * TOK, HD)
        pos = positions(block)
        began = starts <= pos
        left = ends > pos
        start = jnp.max(jnp.where(began, starts, 0.0), axis=1, keepdims=True)
        end = jnp.min(jnp.where(left, ends, 4096.0), axis=1, keepdims=True)
        page = jnp.sum(jnp.where(began & left, page_row, 0.0), axis=1, keepdims=True)
        scale = HD**-0.5
        near = lax.dot_general(query, keys, contract_last, preferred_element_type=F32) * scale
        paged = lax.dot_general(query, page_keys, contract_last, preferred_element_type=F32)
        own = paged[:, 0:PAGE]
        for n in range(1, NQ):
            own = jnp.where(page == float(n), paged[:, n * PAGE : (n + 1) * PAGE], own)
        own = own * scale
        key_pos = (first * TOK).astype(F32) + iota_f((TOK, 3 * TOK), 1)
        visible = (key_pos >= start) & (key_pos < end)
        near = jnp.where(visible, near, NEG)
        top = jnp.maximum(
            jnp.max(near, axis=1, keepdims=True), jnp.max(own, axis=1, keepdims=True)
        )
        near = jnp.where(visible, jnp.exp(near - top), 0.0)
        own = jnp.exp(own - top)
        total = jnp.sum(near, axis=1, keepdims=True) + jnp.sum(own, axis=1, keepdims=True)
        spread = jnp.concatenate(
            [jnp.where(page == float(n), own, 0.0).astype(BF16) for n in range(NQ)], axis=1
        )
        weighted = jnp.dot(near.astype(BF16), values, preferred_element_type=F32)
        weighted = weighted + jnp.dot(spread, page_values, preferred_element_type=F32)
        attn_stage[block] = (weighted / total).astype(BF16)

        @pl.when(i < 15)
        def _():
            attn_copy(block).start()

    attn[:, my_col] = attn_stage[me]

    @pl.loop(1, 16)
    def _(i):
        src = (me - i + 16) % 16
        col = pl.ds(pl.multiple_of(src * HD, HD), HD)
        remote(
            attn_stage.at[src], attn.at[:, col], attn_s.at[src], attn_r.at[src], sibling
        ).wait_recv()

    square = jnp.zeros((TOK, 1), F32)
    for n in range(NWO):
        cols = slice(n * WO, (n + 1) * WO)
        wo_copy(n).wait()
        mixed = jnp.dot(attn[...], wo_buf[n % 3], preferred_element_type=F32)
        summed = (hidden[:, cols].astype(F32) + mixed).astype(BF16)
        resid[:, cols] = summed
        wide = summed.astype(F32)
        square = square + jnp.sum(wide * wide, axis=1, keepdims=True)
        if n + 3 < NWO:
            wo_copy(n + 3).start()
    inverse = lax.rsqrt(square * (1.0 / D) + EPS)
    my_rows = pl.ds(pl.multiple_of(z * TOK, TOK), TOK)

    mate = z + 1 - 2 * (z % 2)
    across = 3 - z

    def tok_copy(c, hop):
        owner = mate if hop == 2 and c > 1 else z
        rows = pl.ds(pl.multiple_of(owner * TOK, TOK), TOK)
        block = tok.at[rows, pl.ds(c * CH, CH)]
        return remote(
            block, block, tok_s.at[c, hop], tok_r.at[c, hop],
            peer(x, y, (mate, across, across if c > 1 else (z + 2) % 4)[hop], core),
        )

    def tok_arrival(c, hop):
        owner = (mate, across, 3 - mate)[hop]
        rows = pl.ds(pl.multiple_of(owner * TOK, TOK), TOK)
        block = tok.at[rows, pl.ds(c * CH, CH)]
        remote(block, block, tok_s.at[c, hop], tok_r.at[c, hop], sibling).wait_recv()

    for c in range(NCH):
        cols = slice(c * CH, (c + 1) * CH)
        tok[my_rows, cols] = (resid[:, cols].astype(F32) * inverse * moe_gain[:, cols]).astype(BF16)
        for hop in range(3 if c < 2 else 2):
            tok_copy(c, hop).start()

    @pl.when(jnp.logical_not(kappa))
    def _():
        for n in range(3):
            cross_weight(n).start()

    def row_block(r):
        return pl.ds(pl.multiple_of(r * ROWS, ROWS), ROWS)

    def disp_copy(r, c):
        rows = row_block(r)
        cols = pl.ds(c * CH, CH)
        return remote(
            stage.at[rows, cols], arrive.at[rows, cols], disp_s.at[r, c], disp_r.at[r, c],
            peer((x + pick(OFFSETS, 0, r)) % 4, (y + pick(OFFSETS, 1, r)) % 4, z, core),
        )

    def select_rows(g, c):
        rows = pl.ds(pl.multiple_of(g * 4 * ROWS, 4 * ROWS), 4 * ROWS)
        cols = slice(c * CH, (c + 1) * CH)
        picked = jnp.dot(sel[rows, :], tok[:, cols], preferred_element_type=F32)
        stage[rows, cols] = picked.astype(BF16)

    def not_self(r, action):
        if isinstance(r, int):
            if r != SELF:
                action()
        else:
            pl.when(r != SELF)(action)

    def disp_group(g, act_on):
        for i in range(4):
            def action(r=g * 4 + i):
                for c in range(NCH):
                    act_on(disp_copy(r, c))

            not_self(g * 4 + i, action)

    for c in range(NCH):
        cols = slice(c * CH, (c + 1) * CH)
        tok_arrival(c, 0)
        if c > 1:
            tok_copy(c, 2).start()
        tok_arrival(c, 1)
        tok_arrival(c, 2)
        select_rows(0, c)
        for i in range(4):
            disp_copy(i, c).start()

    @pl.loop(1, 4)
    def _(g):
        for c in range(NCH):
            select_rows(g, c)
            for i in range(4):
                not_self(g * 4 + i, lambda r=g * 4 + i: disp_copy(r, c).start())

    self_rows = slice(SELF * ROWS, (SELF + 1) * ROWS)
    arrive[self_rows, :] = stage[self_rows, :]

    def near_weight(n):
        @pl.when(kappa)
        def _():
            local_weight(n).wait()

        @pl.when(jnp.logical_not(kappa))
        def _():
            first_weight(n).wait_recv()

    def far_weight(n):
        @pl.when(kappa)
        def _():
            cross_weight(n).wait_recv()
            second_weight(n).start()

        @pl.when(jnp.logical_not(kappa))
        def _():
            second_weight(n).wait_recv()

    for n in range(2):
        near_weight(n)
        far_weight(n)

    @pl.loop(0, 4)
    def _(g):
        disp_group(g, lambda copy: copy.wait_recv())
        rows = pl.ds(pl.multiple_of(g * 4 * ROWS, 4 * ROWS), 4 * ROWS)
        for s in range(2):
            gate = jnp.dot(arrive[rows, :], gate_b[s], preferred_element_type=F32)
            up = jnp.dot(arrive[rows, :], up_b[s], preferred_element_type=F32)
            act[rows, s * FFH : (s + 1) * FFH] = (
                gate * (1.0 / (1.0 + jnp.exp(-gate))) * up
            ).astype(BF16)

    def ret_copy(r, c):
        rows = row_block(r)
        cols = pl.ds(c * CH, CH)
        return remote(
            arrive.at[rows, cols], ret.at[rows, cols], ret_s.at[r, c], ret_r.at[r, c],
            peer((x - pick(OFFSETS, 0, r) + 4) % 4, (y - pick(OFFSETS, 1, r) + 4) % 4, z, core),
        )

    def ret_chunk(c, act_on):
        @pl.loop(0, PLANE)
        def _(r):
            not_self(r, lambda: act_on(ret_copy(r, c)))

    def down_rows(c):
        cols = slice(c * CH, (c + 1) * CH)

        @pl.loop(0, 4)
        def _(g):
            rows = pl.ds(pl.multiple_of(g * 4 * ROWS, 4 * ROWS), 4 * ROWS)
            piece = jnp.dot(act[rows, 0:FFH], down_b[0, :, cols], preferred_element_type=F32)
            piece = piece + jnp.dot(
                act[rows, FFH : 2 * FFH], down_b[1, :, cols], preferred_element_type=F32
            )
            arrive[rows, cols] = piece.astype(BF16)

        ret[self_rows, cols] = arrive[self_rows, cols]

    def part_copy(c, dz):
        target = (z + dz) % 4
        rows = pl.ds(pl.multiple_of(target * TOK, TOK), TOK)
        return remote(
            part_stage.at[c, rows, :], part_in.at[c, dz - 1],
            part_s.at[c, dz - 1], part_r.at[c, dz - 1], peer(x, y, target, core),
        )

    def combine(c):
        cols = slice(c * CH, (c + 1) * CH)

        ret_chunk(c, lambda copy: copy.wait_recv())
        sums = lax.dot_general(
            wsel[...], ret[:, cols], (((0,), (0,)), ((), ())), preferred_element_type=F32
        )
        part_stage[c] = sums.astype(BF16)
        for dz in (1, 3, 2):
            part_copy(c, dz).start()
        part[...] = sums
        return part[my_rows, :]

    def finish(c, own, score):
        cols = slice(c * CH, (c + 1) * CH)
        total = own
        for dz in range(1, 4):
            part_copy(c, dz).wait_recv()
            total = total + part_in[c, dz - 1].astype(F32)
        out = (resid[:, cols].astype(F32) + total).astype(BF16)
        lay[:, cols] = out
        return score + jnp.sum(out.astype(F32) * score_w[:, cols], axis=1, keepdims=True)

    def send_back(c):
        ret_chunk(c, lambda copy: copy.start())

    def sent_back(c):
        ret_chunk(c, lambda copy: copy.wait_send())

    near_weight(2)
    far_weight(2)
    score = jnp.zeros((TOK, 1), F32)
    own = {}
    for step in range(NCH + 3):
        if step < NCH:
            down_rows(step)
            if step >= 2:
                sent_back(step - 2)
            send_back(step)
        if 2 <= step < NCH + 2:
            own[step - 2] = combine(step - 2)
        if step >= 3:
            score = finish(step - 3, own.pop(step - 3), score)

    member = (starts <= own_pos) & (ends > own_pos)
    sums = jnp.sum(jnp.where(member, score, 0.0), axis=0, keepdims=True)
    dsum[me, :, 0:DOCS] = jnp.broadcast_to(sums, (8, DOCS))
    dsum[me, :, DOCS:128] = jnp.zeros((8, 128 - DOCS), F32)

    def dsum_copy(target):
        return remote(dsum.at[me], dsum.at[me], dsum_s.at[target], dsum_r.at[me], (req, target))

    @pl.loop(1, 16)
    def _(i):
        dsum_copy((me + i) % 16).start()

    for dz in range(1, 4):
        meta_copy(dz).wait_send()
    for n in range(3):
        @pl.when(kappa)
        def _():
            first_weight(n).wait_send()
            second_weight(n).wait_send()

        @pl.when(jnp.logical_not(kappa))
        def _():
            cross_weight(n).wait_send()

    @pl.loop(1, 16)
    def _(i):
        head_copy((me + i) % 16).wait_send()
        attn_copy((me + i) % 16).wait_send()

    for c in range(NCH):
        for n in range(3):
            tok_copy(c, n).wait_send()
            part_copy(c, n + 1).wait_send()

    @pl.loop(0, 4)
    def _(g):
        disp_group(g, lambda copy: copy.wait_send())

    sent_back(NCH - 2)
    sent_back(NCH - 1)

    @pl.loop(1, 16)
    def _(i):
        src = (me - i + 16) % 16
        remote(
            dsum.at[src], dsum.at[src], dsum_s.at[src], dsum_r.at[src], sibling
        ).wait_recv()

    whole = dsum[0]
    for n in range(1, 16):
        whole = whole + dsum[n]
    doc_out[...] = whole[0:1, 0:DOCS] / len_row

    @pl.loop(1, 16)
    def _(i):
        dsum_copy((me + i) % 16).wait_send()


def local(
    hidden_in, qkv, q_gain, k_gain, query_pages, page_table, doc_lengths, doc_query, out_weight,
    moe_gain, routes, route_weight, gate_weight, up_weight, down_weight, score_weight,
):
    half = ROPE_BASE ** (-(np.arange(HD // 2, dtype=np.float32) * 2.0 / HD))
    freq = jnp.asarray(np.concatenate([half, half])[None].astype(np.float32))
    vmem = pl.BlockSpec(memory_space=pltpu.VMEM)
    hbm = pl.BlockSpec(memory_space=pl.ANY)
    dma = pltpu.SemaphoreType.DMA
    call = pl.pallas_call(
        kernel,
        out_shape=(
            jax.ShapeDtypeStruct((TOK, D), BF16),
            jax.ShapeDtypeStruct((1, DOCS), F32),
        ),
        in_specs=[
            vmem, vmem, vmem, vmem, vmem, vmem, vmem, vmem, hbm, vmem, vmem, vmem,
            hbm, hbm, hbm, vmem, vmem,
        ],
        out_specs=(vmem, vmem),
        scratch_shapes=[
            pltpu.VMEM((HEADS, TOK, 3 * HD), BF16),
            pltpu.VMEM((HEADS, TOK, 3 * HD), BF16),
            pltpu.VMEM((TOK, D), BF16),
            pltpu.VMEM((HEADS, TOK, HD), BF16),
            pltpu.VMEM((3, D, WO), BF16),
            pltpu.VMEM((2, D, FFH), BF16),
            pltpu.VMEM((2, D, FFH), BF16),
            pltpu.VMEM((2, FFH, D), BF16),
            pltpu.VMEM((LINE, 16, TOK), F32),
            pltpu.VMEM((LINE * TOK, LINE * TOK), BF16),
            pltpu.VMEM((PLANE, LINE * TOK), F32),
            pltpu.VMEM((PLANE, LINE * TOK), F32),
            pltpu.VMEM((PLANE * ROWS, LINE * TOK), BF16),
            pltpu.VMEM((PLANE * ROWS, LINE * TOK), BF16),
            pltpu.VMEM((TOK, D), BF16),
            pltpu.VMEM((LINE * TOK, D), BF16),
            pltpu.VMEM((PLANE * ROWS, D), BF16),
            pltpu.VMEM((PLANE * ROWS, D), BF16),
            pltpu.VMEM((PLANE * ROWS, 2 * FFH), BF16),
            pltpu.VMEM((PLANE * ROWS, D), BF16),
            pltpu.VMEM((LINE * TOK, CH), F32),
            pltpu.VMEM((NCH, LINE * TOK, CH), BF16),
            pltpu.VMEM((NCH, LINE - 1, TOK, CH), BF16),
            pltpu.VMEM((16, 8, 128), F32),
            dma((16,)), dma((16,)), dma((16,)), dma((16,)), dma((3,)),
            dma((3,)), dma((3,)), dma((3,)), dma((3,)), dma((3,)), dma((3,)), dma((3,)),
            dma((NCH, 3)), dma((NCH, 3)),
            dma((PLANE, NCH)), dma((PLANE, NCH)), dma((PLANE, NCH)), dma((PLANE, NCH)),
            dma((NCH, 3)), dma((NCH, 3)), dma((16,)), dma((16,)),
        ],
        compiler_params=pltpu.CompilerParams(
            collective_id=0, has_side_effects=True, vmem_limit_bytes=60 * 1024 * 1024
        ),
        cost_estimate=pl.CostEstimate(
            flops=26_000_000_000, bytes_accessed=20_000_000, transcendentals=3_000_000
        ),
    )
    return call(
        hidden_in, qkv, q_gain[None], k_gain[None], query_pages[0], page_table, doc_lengths,
        doc_query, out_weight, moe_gain[None], routes, route_weight, gate_weight, up_weight, down_weight,
        score_weight[None], freq,
    )


def solution(mesh):
    rows = P(("req", "exp"), None)
    blocks = P(("req", "exp"), None, None)
    in_specs = (
        rows, rows, P(), P(), P("req", None, None, "exp"), P("req", None), P("req", None),
        P("req", None), P(), P(), rows, rows, blocks, blocks, blocks, P(),
    )
    out_specs = (rows, P("req", None))
    return jax.shard_map(local, mesh=mesh, in_specs=in_specs, out_specs=out_specs, check_vma=False)
```
